128 devices in a mesh: replica: 4 (over y_lo, core), fsdp: 32 (over y_hi, x, z).
Axes of the slice: x: 4, y: 4 (y_hi: 2, y_lo: 2; y = y_hi * 2 + y_lo), z: 4, core: 2. Of those that a mesh axis runs over, the one named last changes fastest.
Arguments:
- activations: bfloat16 [4, 16384, 4096], P('replica', 'fsdp'), may hold values from -6 to 6
- kv_cotangent: bfloat16 [4, 16384, 1024], P('replica', 'fsdp'), may hold values from -6 to 6
- kv_master: float32 [4, 4096, 1024], P('replica', 'fsdp'), may hold values from -0.09375 to 0.09375
- kv_first: float32 [4, 4096, 1024], P('replica', 'fsdp'), may hold values from -6 to 6
- kv_second: float32 [4, 4096, 1024], P('replica', 'fsdp'), may hold values from 0.25 to 4
- outer_params: float32 [2, 1024, 4096], P(None, 'fsdp'), may hold values from -6 to 6
- local_params: float32 [4, 2, 1024, 4096], P('replica', None, 'fsdp'), may hold values from -6 to 6
- outer_momentum: float32 [2, 1024, 4096], P(None, 'fsdp'), may hold values from -6 to 6
Outputs:
- kv_output: bfloat16 [4, 16384, 1024], P('replica', 'fsdp')
- input_grad: bfloat16 [4, 16384, 4096], P('replica', 'fsdp')
- new_master: float32 [4, 4096, 1024], P('replica', 'fsdp')
- new_first: float32 [4, 4096, 1024], P('replica', 'fsdp')
- new_second: float32 [4, 4096, 1024], P('replica', 'fsdp')
- new_outer: float32 [2, 1024, 4096], P(None, 'fsdp')
- new_momentum: float32 [2, 1024, 4096], P(None, 'fsdp')
The draws below stay inside these ranges and needn't reach their ends.
All inputs are finite; a program needn't handle non-finite values.
Results may differ from the reference program's by a relative error of at most 0.019.
Values may be sent and summed in bfloat16 or wider, within the bound.
A program may use at most 128 MiB of HBM per device.

```python
import math
import jax
import jax.numpy as jnp
from jax import lax

D = 4096
KVD = 512
TOK_DEV = 512
TOKENS = 16384
FRAG_LAYERS = 2
FRAG_ROWS = 1024
N_REPLICA = 4
N_FSDP = 32


def strengthened(drawn, stream_key, source, target, blocks, factor):
    def block_of(dim):
        return (jnp.arange(drawn.shape[dim]) // (drawn.shape[dim] // blocks)).reshape((-1,) + (1,) * (drawn.ndim - 1 - dim))

    one_side = jax.random.permutation(stream_key, blocks)[block_of(target)]
    other_side = (block_of(target) + blocks // 2) % blocks
    return jnp.where((block_of(source) == one_side) | (block_of(source) == other_side), factor * drawn, drawn)


def level_of(rng, extent, cuts, least, top_value):
    level = 1.0
    for axis_at, blocks in cuts:
        draws = jax.random.uniform(jax.random.fold_in(jax.random.fold_in(rng, 6), axis_at), (blocks,), jnp.float32, least / len(cuts), top_value / len(cuts))
        level = level * jnp.repeat(jnp.exp(draws), extent[axis_at] // blocks).reshape((-1,) + (1,) * (len(extent) - 1 - axis_at))
    return level


def gaussian(rng, shape, width, bound, pieces=(), held_as=jnp.bfloat16):
    drawn = jax.random.normal(rng, shape, jnp.float32) * width
    if len(pieces) > 0:
        drawn = level_of(rng, shape, pieces, -0.22, 0.18) * drawn
    return jnp.clip(drawn, min=-bound, max=bound).astype(held_as)


def noise_with(key, shape, deviation, reach, split, heavy, kind=jnp.bfloat16):
    array = deviation * jax.random.normal(key, shape, jnp.float32)
    if split:
        array = array * level_of(key, shape, split, -0.22, 0.18)
    return jnp.clip(strengthened(array, jax.random.fold_in(key, 3), *heavy), -reach, reach).astype(kind)


def setup_inputs(seed: int = 0) -> dict:
    keys = jax.random.split(jax.random.key(seed), 9)
    return {
        "activations": noise_with(keys[0], (N_REPLICA, TOKENS, D), 1.0, 6.0, ((0, 4), (1, 32)), (1, 2, 32, 2.75)),
        "kv_cotangent": gaussian(keys[1], (N_REPLICA, TOKENS, 2 * KVD), 1.0, 6.0, ((0, 4), (1, 32))),
        "kv_master": gaussian(keys[2], (N_REPLICA, D, 2 * KVD), D ** -0.5, 0.09375, ((0, 4), (1, 32)), jnp.float32),
        "kv_first": gaussian(keys[3], (N_REPLICA, D, 2 * KVD), 1.0, 6.0, ((0, 4), (1, 32)), jnp.float32),
        "kv_second": jnp.clip(jnp.exp(math.log(4.0) - 2.7725887 * jax.random.uniform(keys[4], (N_REPLICA, D, 2 * KVD), jnp.float32) ** level_of(keys[4], (N_REPLICA, D, 2 * KVD), ((0, 4), (1, 32)), -0.2, 0.2)), 0.25, 4.0),
        "outer_params": gaussian(keys[5], (FRAG_LAYERS, FRAG_ROWS, D), 1.0, 6.0, ((1, 32),), jnp.float32),
        "local_params": gaussian(keys[6], (N_REPLICA, FRAG_LAYERS, FRAG_ROWS, D), 1.0, 6.0, ((0, 4), (2, 32)), jnp.float32),
        "outer_momentum": gaussian(keys[7], (FRAG_LAYERS, FRAG_ROWS, D), 1.0, 6.0, ((1, 32),), jnp.float32),
    }


FIRST_DECAY = 0.9
SECOND_DECAY = 0.95
ADAM_STEPS = 20.0
ADAM_EPSILON = 1e-08
INNER_RATE = 0.01
WEIGHT_DECAY = 0.1
NESTEROV = 0.9
OUTER_RATE = 0.7

def adam_update(master, first, second, grad):
    first = FIRST_DECAY * first + (1.0 - FIRST_DECAY) * grad
    second = SECOND_DECAY * second + (1.0 - SECOND_DECAY) * grad * grad
    first_fix = 1.0 - FIRST_DECAY ** ADAM_STEPS
    second_fix = 1.0 - SECOND_DECAY ** ADAM_STEPS
    update = first / first_fix / (jnp.sqrt(second / second_fix) + ADAM_EPSILON)
    master = master - INNER_RATE * (update + WEIGHT_DECAY * master)
    return (master, first, second)

def replica_pass(activations, cotangent, master, first, second):
    weights = master.astype(jnp.bfloat16)
    projected = jnp.dot(activations, weights, preferred_element_type=jnp.float32).astype(jnp.bfloat16)
    input_grad = jnp.dot(cotangent, weights.T, preferred_element_type=jnp.float32).astype(jnp.bfloat16)
    act_blocks = activations.reshape(N_FSDP, TOK_DEV, D)
    cot_blocks = cotangent.reshape(N_FSDP, TOK_DEV, 2 * KVD)

    def accumulate(summed, pair):
        term = jnp.dot(pair[0].T, pair[1], preferred_element_type=jnp.float32).astype(jnp.bfloat16)
        term = lax.optimization_barrier(term)
        return (summed + term.astype(jnp.float32), None)
    summed, unused = lax.scan(accumulate, jnp.zeros((D, 2 * KVD), jnp.float32), (act_blocks, cot_blocks))
    grad = summed * (1.0 / math.sqrt(TOKENS))
    new_master, new_first, new_second = adam_update(master, first, second, grad)
    return (projected, input_grad, new_master, new_first, new_second)

def reference(activations, kv_cotangent, kv_master, kv_first, kv_second, outer_params, local_params, outer_momentum):
    results = [replica_pass(activations[replica], kv_cotangent[replica], kv_master[replica], kv_first[replica], kv_second[replica]) for replica in range(N_REPLICA)]
    stacked = [jnp.stack([item[slot] for item in results]) for slot in range(5)]
    pseudo = outer_params[None] - local_params
    mean = lax.optimization_barrier(jnp.sum(pseudo, axis=0)) / N_REPLICA
    new_momentum = NESTEROV * outer_momentum + mean
    new_outer = outer_params - OUTER_RATE * (mean + NESTEROV * new_momentum)
    return (stacked[0], stacked[1], stacked[2], stacked[3], stacked[4], new_outer, new_momentum)
```

```python
import math

import jax
import jax.numpy as jnp
from jax import lax
from jax.experimental import pallas as pl
from jax.experimental.pallas import tpu as pltpu
from jax.sharding import PartitionSpec as P

FIRST_DECAY = 0.9
SECOND_DECAY = 0.95
ADAM_STEPS = 20.0
ADAM_EPSILON = 1e-08
INNER_RATE = 0.01
WEIGHT_DECAY = 0.1
NESTEROV = 0.9
OUTER_RATE = 0.7

BF16 = jnp.bfloat16
F32 = jnp.float32
N = 4
ITEMS = 2 * N
LAG_RQ2 = 1
LAG_RS = 2
LAG_GQ2 = 1
LAG_G = 2
ROUNDS = ITEMS + 2


def adam_update(master, first, second, grad):
    first = FIRST_DECAY * first + (1.0 - FIRST_DECAY) * grad
    second = SECOND_DECAY * second + (1.0 - SECOND_DECAY) * grad * grad
    first_fix = 1.0 - FIRST_DECAY**ADAM_STEPS
    second_fix = 1.0 - SECOND_DECAY**ADAM_STEPS
    update = first / first_fix / (jnp.sqrt(second / second_fix) + ADAM_EPSILON)
    master = master - INNER_RATE * (update + WEIGHT_DECAY * master)
    return (master, first, second)


def train_kernel(
    act_hbm,
    cot_hbm,
    master_hbm,
    out_hbm,
    igrad_hbm,
    grad_ref,
    act,
    cot,
    cot_t,
    master,
    w,
    part,
    got_a,
    got_b,
    got_y,
    got_pa,
    got_pb,
    mine,
    acc,
    out,
    igrad,
    load_sem,
    store_sem,
    gp1_s, gp1_r, gp2_s, gp2_r, gy_s, gy_r, gq1_s, gq1_r, gq2_s, gq2_r,
    rq1_s, rq1_r, rq2_s, rq2_r, ry_s, ry_r, rp1_s, rp1_r, rp2_s, rp2_r,
):
    f = lax.axis_index("fsdp")
    y, x, z = f // 16, (f // 4) % 4, f % 4
    first_of = (x, z)
    last_of = (z, x)
    rows = w.shape[1] // 32
    half = rows // 2
    kv = w.shape[2]
    kh = kv // 2
    cols = N * rows

    def device(yy, xx, zz):
        return (yy * 4 + xx) * 4 + zz

    def block(t, yy, p, q):
        return device(yy, p, q) if t == 0 else device(yy, q, p)

    def along_first(t, step):
        return block(t, y, (first_of[t] + step) % 4, last_of[t])

    def along_last(t, step):
        return block(t, y, first_of[t], (last_of[t] + step) % 4)

    partner = device(1 - y, x, z)

    def send_to(src, dst, ss, rs, target):
        return pltpu.make_async_remote_copy(
            src_ref=src, dst_ref=dst, send_sem=ss, recv_sem=rs,
            device_id={"fsdp": target}, device_id_type=pl.DeviceIdType.MESH,
        )

    def w_at(t, b, part_of=None):
        if part_of is None:
            return w.at[t, pl.ds(pl.multiple_of(b * rows, rows), rows)]
        return w.at[t, pl.ds(pl.multiple_of(b * rows + part_of * half, half), half)]

    def sign(d):
        return 1 if d == 0 else 3

    def gp1(t, d):
        own = w_at(t, f)
        return send_to(own, own, gp1_s.at[t, d], gp1_r.at[t, d], along_first(t, sign(d)))

    def gp2(t, d):
        ref = w_at(t, along_first(t, 4 - sign(d)), d)
        return send_to(ref, ref, gp2_s.at[t, d], gp2_r.at[t, d], along_first(t, sign(d)))

    def gy(t, k):
        ref = w_at(t, along_first(t, k))
        return send_to(ref, ref, gy_s.at[t, k], gy_r.at[t, k], partner)

    def gather_item(t, i):
        plane = (y + i // 4) % 2
        return plane, (first_of[t] + i) % 4

    def gq1(t, i, d):
        plane, p = gather_item(t, i)
        ref = w_at(t, block(t, plane, p, last_of[t]))
        return send_to(ref, ref, gq1_s.at[t, i, d], gq1_r.at[t, i, d], along_last(t, sign(d)))

    def gq2(t, i, d):
        plane, p = gather_item(t, i)
        ref = w_at(t, block(t, plane, p, (last_of[t] + 4 - sign(d)) % 4), d)
        return send_to(ref, ref, gq2_s.at[t, i, d], gq2_r.at[t, i, d], along_last(t, sign(d)))

    def reduce_item(t, i):
        plane = (y + 1 + i // 4) % 2
        return plane, (first_of[t] + i + 1) % 4

    def part_at(t, i, q, part_of=None):
        ref = part.at[t, i, q]
        return ref if part_of is None else ref.at[pl.ds(part_of * kh, kh)]

    def rq1(t, i, d):
        return send_to(
            part_at(t, i, (last_of[t] + 2) % 4, d), got_a.at[t, i, d],
            rq1_s.at[t, i, d], rq1_r.at[t, i, d], along_last(t, sign(d)),
        )

    def rq2(t, i, d):
        return send_to(
            part_at(t, i, (last_of[t] + sign(d)) % 4), got_b.at[t, i, d],
            rq2_s.at[t, i, d], rq2_r.at[t, i, d], along_last(t, sign(d)),
        )

    def ry(t, k):
        return send_to(
            part_at(t, k, last_of[t]), got_y.at[t, k], ry_s.at[t, k], ry_r.at[t, k], partner
        )

    def rp1(t, d):
        return send_to(
            part_at(t, 5, last_of[t], d), got_pa.at[t, d],
            rp1_s.at[t, d], rp1_r.at[t, d], along_first(t, sign(d)),
        )

    def rp2(t, d):
        return send_to(
            part_at(t, 4 if d == 0 else 6, last_of[t]), got_pb.at[t, d],
            rp2_s.at[t, d], rp2_r.at[t, d], along_first(t, sign(d)),
        )

    types = (0, 1)
    ways = (0, 1)

    load_master = pltpu.make_async_copy(master_hbm.at[0], master, load_sem.at[0])
    load_cot = pltpu.make_async_copy(cot_hbm.at[0], cot, load_sem.at[1])
    plane_cols = act.shape[1] // 2

    def load_act(plane, slot):
        at = pl.ds(pl.multiple_of(plane * plane_cols, plane_cols), plane_cols)
        return pltpu.make_async_copy(act_hbm.at[0, :, at], act.at[:, at], load_sem.at[slot])

    load_master.start()
    load_cot.start()
    load_act(1 - y, 2).start()
    load_act(y, 3).start()

    barrier = pltpu.get_barrier_semaphore()
    around = [along_first(0, 1), along_first(0, 3), along_last(0, 1), along_last(0, 3), partner]
    for other in around:
        pl.semaphore_signal(
            barrier, inc=1, device_id={"fsdp": other}, device_id_type=pl.DeviceIdType.MESH
        )
    load_master.wait()
    own_rows = pl.ds(pl.multiple_of(f * rows, rows), rows)
    for t in types:
        w[t, own_rows, :] = master[:, t * kv:(t + 1) * kv].astype(BF16)
    pl.semaphore_wait(barrier, len(around))
    for t in types:
        for d in ways:
            gp1(t, d).start()
    for t in types:
        for d in ways:
            gq1(t, 0, d).start()
        gy(t, 0).start()

    load_cot.wait()
    for t in types:
        cot_t[pl.ds(t * kv, kv), :] = cot[:, t * kv:(t + 1) * kv].T
    for t in types:
        acc[t] = jnp.zeros(acc.shape[1:], F32)
    load_act(1 - y, 2).wait()

    def make_parts(i):
        for t in types:
            plane, p = reduce_item(t, i)
            if t == 0:
                at = pl.multiple_of((plane * 4 + p) * cols, cols)
                right = act[:, pl.ds(at, cols)]
            else:
                right = jnp.concatenate(
                    [
                        act[:, pl.ds(pl.multiple_of(device(plane, q, p) * rows, rows), rows)]
                        for q in range(N)
                    ],
                    axis=1,
                )
            for m in range(2):
                at = m * kh
                prod = jnp.dot(
                    cot_t[pl.ds(t * kv + at, kh), :], right, preferred_element_type=F32
                ).astype(BF16)
                for q in range(N):
                    part[t, i, q, pl.ds(at, kh), :] = prod[:, q * rows:(q + 1) * rows]

    def add_half(t, i, d, got):
        at = pl.ds(d * kh, kh)
        q = (last_of[t] + sign(d)) % 4
        total = part[t, i, q, at, :].astype(F32) + got[...].astype(F32)
        part[t, i, q, at, :] = total.astype(BF16)

    def project(i):
        for t in types:
            plane, p = gather_item(t, i)
            if t == 0:
                at = pl.multiple_of((plane * 4 + p) * cols, cols)
                left = act[:, pl.ds(at, cols)]
                right = w[t, pl.ds(at, cols), :]
            else:
                spans = [
                    pl.ds(pl.multiple_of(device(plane, q, p) * rows, rows), rows) for q in range(N)
                ]
                left = jnp.concatenate([act[:, s] for s in spans], axis=1)
                right = jnp.concatenate([w[t, s, :] for s in spans], axis=0)
            acc[t] += jnp.dot(left, right, preferred_element_type=F32)

    def store_igrad(b):
        at = pl.ds(pl.multiple_of(b * cols, cols), cols)
        return pltpu.make_async_copy(igrad.at[:, at], igrad_hbm.at[0, :, at], store_sem.at[b])

    def input_grads(plane):
        def one(k, carry):
            b = plane * 4 + k
            at = pl.ds(pl.multiple_of(b * cols, cols), cols)
            total = None
            for t in types:
                term = lax.dot_general(
                    cot[:, t * kv:(t + 1) * kv], w[t, at, :], (((1,), (1,)), ((), ())),
                    preferred_element_type=F32,
                )
                total = term if total is None else total + term
            igrad[:, at] = total.astype(BF16)
            store_igrad(b).start()
            return carry

        lax.fori_loop(0, N, one, 0)

    def round_of(r, carry):
        @pl.when(r == 1)
        def _():
            for t in types:
                for d in (1, 0):
                    gp1(t, d).wait_recv()
                    gp2(t, d).start()
                gy(t, 1).start()
                gy(t, 3).start()

        @pl.when(r == 2)
        def _():
            for t in types:
                for d in ways:
                    gp2(t, d).wait_recv()
                gy(t, 2).start()

        @pl.when((r >= 4) & (r < ITEMS))
        def _():
            for t in types:
                gy(t, r % 4).wait_recv()

        @pl.when((r >= 1) & (r < ITEMS))
        def _():
            for t in types:
                for d in ways:
                    gq1(t, r, d).start()

        @pl.when(r == LAG_G)
        def _():
            load_act(y, 3).wait()

        @pl.when(r < ITEMS)
        def _():
            make_parts(r)
            for t in types:
                for d in ways:
                    rq1(t, r, d).start()

        @pl.when((r >= LAG_RQ2) & (r < ITEMS + LAG_RQ2))
        def _():
            i = r - LAG_RQ2
            for t in types:
                for d in ways:
                    rq1(t, i, d).wait_recv()
                    add_half(t, i, d, got_a.at[t, i, d])
                    rq2(t, i, d).start()

        @pl.when((r >= LAG_GQ2) & (r < ITEMS + LAG_GQ2))
        def _():
            i = r - LAG_GQ2
            for t in types:
                for d in ways:
                    gq1(t, i, d).wait_recv()
                    gq2(t, i, d).start()

        @pl.when((r >= LAG_RS) & (r < ITEMS + LAG_RS))
        def _():
            i = r - LAG_RS
            for t in types:
                for d in ways:
                    rq2(t, i, d).wait_recv()
                q = last_of[t]
                mine[t] = (
                    part[t, i, q].astype(F32)
                    + got_b[t, i, 0].astype(F32)
                    + got_b[t, i, 1].astype(F32)
                )

                @pl.when(i < 4)
                def _():
                    part[t, i, q] = mine[t].astype(BF16)
                    ry(t, i).start()

                @pl.when(i >= 4)
                def _():
                    ry(t, i % 4).wait_recv()
                    mine[t] += got_y[t, i % 4].astype(F32)

                @pl.when((i >= 4) & (i < 7))
                def _():
                    part[t, i, q] = mine[t].astype(BF16)

            @pl.when(i == 5)
            def _():
                for t in types:
                    for d in ways:
                        rp1(t, d).start()

            @pl.when(i == 6)
            def _():
                for t in types:
                    for d in ways:
                        rp1(t, d).wait_recv()
                        at = pl.ds(d * kh, kh)
                        k = 4 if d == 0 else 6
                        total = part[t, k, last_of[t], at, :].astype(F32)
                        total += got_pa[t, d].astype(F32)
                        part[t, k, last_of[t], at, :] = total.astype(BF16)
                        rp2(t, d).start()

        @pl.when((r >= LAG_G) & (r < ITEMS + LAG_G))
        def _():
            i = r - LAG_G
            for t in types:
                for d in ways:
                    gq2(t, i, d).wait_recv()
            project(i)

            @pl.when(i == 3)
            def _():
                input_grads(y)

            @pl.when(i == 7)
            def _():
                input_grads(1 - y)

        return carry

    lax.fori_loop(0, ROUNDS, round_of, 0)

    for t in types:
        out[:, t * kv:(t + 1) * kv] = acc[t].astype(BF16)
    store_out = pltpu.make_async_copy(out, out_hbm.at[0], store_sem.at[8])
    store_out.start()
    for t in types:
        for d in ways:
            rp2(t, d).wait_recv()
        total = mine[t] + got_pb[t, 0].astype(F32) + got_pb[t, 1].astype(F32)
        grad_ref[:, t * kv:(t + 1) * kv] = total.T

    for t in types:
        for d in ways:
            gp1(t, d).wait_send()
            gp2(t, d).wait_send()
            rp1(t, d).wait_send()
            rp2(t, d).wait_send()

    def drain_four(k, carry):
        for t in types:
            gy(t, k).wait_send()
            ry(t, k).wait_send()
        return carry

    def drain_eight(i, carry):
        for t in types:
            for d in ways:
                gq1(t, i, d).wait_send()
                gq2(t, i, d).wait_send()
                rq1(t, i, d).wait_send()
                rq2(t, i, d).wait_send()
        store_igrad(i).wait()
        return carry

    lax.fori_loop(0, N, drain_four, 0)
    lax.fori_loop(0, ITEMS, drain_eight, 0)
    store_out.wait()


def train_step(activations, cotangent, master):
    tok, width = activations.shape[1:]
    kv2 = cotangent.shape[2]
    rows = master.shape[1]
    kv, kh = kv2 // 2, kv2 // 4
    dma = pltpu.SemaphoreType.DMA
    sems = []
    for shape in ((2, 2), (2, 2), (2, 4), (2, 8, 2), (2, 8, 2)):
        sems += [dma(shape), dma(shape)]
    for shape in ((2, 8, 2), (2, 8, 2), (2, 4), (2, 2), (2, 2)):
        sems += [dma(shape), dma(shape)]
    hbm = pl.BlockSpec(memory_space=pl.ANY)
    return pl.pallas_call(
        train_kernel,
        out_shape=(
            jax.ShapeDtypeStruct((1, tok, kv2), BF16),
            jax.ShapeDtypeStruct((1, tok, width), BF16),
            jax.ShapeDtypeStruct((rows, kv2), F32),
        ),
        in_specs=[hbm, hbm, hbm],
        out_specs=(hbm, hbm, pl.BlockSpec(memory_space=pltpu.VMEM)),
        scratch_shapes=[
            pltpu.VMEM((tok, width), BF16),
            pltpu.VMEM((tok, kv2), BF16),
            pltpu.VMEM((kv2, tok), BF16),
            pltpu.VMEM((rows, kv2), F32),
            pltpu.VMEM((2, width, kv), BF16),
            pltpu.VMEM((2, 8, 4, kv, rows), BF16),
            pltpu.VMEM((2, 8, 2, kh, rows), BF16),
            pltpu.VMEM((2, 8, 2, kv, rows), BF16),
            pltpu.VMEM((2, 4, kv, rows), BF16),
            pltpu.VMEM((2, 2, kh, rows), BF16),
            pltpu.VMEM((2, 2, kv, rows), BF16),
            pltpu.VMEM((2, kv, rows), F32),
            pltpu.VMEM((2, tok, kv), F32),
            pltpu.VMEM((tok, kv2), BF16),
            pltpu.VMEM((tok, width), BF16),
            dma((4,)),
            dma((9,)),
            *sems,
        ],
        compiler_params=pltpu.CompilerParams(
            collective_id=0, has_side_effects=True, vmem_limit_bytes=56 * 2**20
        ),
        cost_estimate=pl.CostEstimate(
            flops=6 * tok * width * kv2, bytes_accessed=100 * 2**20, transcendentals=0
        ),
        name="train_step",
    )(activations, cotangent, master)


def shards(
    activations,
    kv_cotangent,
    kv_master,
    kv_first,
    kv_second,
    outer_params,
    local_params,
    outer_momentum,
):
    pseudo = outer_params - local_params[0]
    replicas = lax.axis_size("replica")
    summed_pseudo = lax.psum(pseudo.astype(BF16), "replica").astype(F32)

    projected, input_grad, summed = train_step(activations, kv_cotangent, kv_master)
    all_tokens = activations.shape[1] * lax.axis_size("fsdp")
    grad = summed * (1.0 / math.sqrt(all_tokens))
    new_master, new_first, new_second = adam_update(
        kv_master[0], kv_first[0], kv_second[0], grad
    )

    mean = summed_pseudo / replicas
    new_momentum = NESTEROV * outer_momentum + mean
    new_outer = outer_params - OUTER_RATE * (mean + NESTEROV * new_momentum)
    return (
        projected,
        input_grad,
        new_master[None],
        new_first[None],
        new_second[None],
        new_outer,
        new_momentum,
    )


def solution(mesh):
    row_split = P("replica", "fsdp", None)
    fragment = P(None, "fsdp", None)
    return jax.shard_map(
        shards,
        mesh=mesh,
        in_specs=(
            row_split,
            row_split,
            row_split,
            row_split,
            row_split,
            fragment,
            P("replica", None, "fsdp", None),
            fragment,
        ),
        out_specs=(row_split, row_split, row_split, row_split, row_split, fragment, fragment),
        check_vma=False,
    )
```

```python
import math

import jax
import jax.numpy as jnp
from jax import lax
from jax.experimental import pallas as pl
from jax.experimental.pallas import tpu as pltpu
from jax.sharding import PartitionSpec as P

FIRST_DECAY = 0.9
SECOND_DECAY = 0.95
ADAM_STEPS = 20.0
ADAM_EPSILON = 1e-08
INNER_RATE = 0.01
WEIGHT_DECAY = 0.1
NESTEROV = 0.9
OUTER_RATE = 0.7

BF16 = jnp.bfloat16
F32 = jnp.float32
N_REPLICA = 4
N = 4
ITEMS = 2 * N
LAG_RQ2 = 1
LAG_RS = 2
LAG_GQ2 = 1
LAG_G = 2
ROUNDS = ITEMS + 2


def adam_update(master, first, second, grad):
    first = FIRST_DECAY * first + (1.0 - FIRST_DECAY) * grad
    second = SECOND_DECAY * second + (1.0 - SECOND_DECAY) * grad * grad
    first_fix = 1.0 - FIRST_DECAY**ADAM_STEPS
    second_fix = 1.0 - SECOND_DECAY**ADAM_STEPS
    update = first / first_fix / (jnp.sqrt(second / second_fix) + ADAM_EPSILON)
    master = master - INNER_RATE * (update + WEIGHT_DECAY * master)
    return (master, first, second)


def train_kernel(
    act_hbm,
    cot_hbm,
    master_hbm,
    outer_hbm,
    local_hbm,
    moment_hbm,
    out_hbm,
    igrad_hbm,
    grad_ref,
    new_outer_hbm,
    new_moment_hbm,
    act,
    cot,
    cot_t,
    master,
    w,
    part,
    got_a,
    got_b,
    got_y,
    got_pa,
    got_pb,
    mine,
    acc,
    out,
    igrad,
    outer,
    local,
    moment,
    pseudo,
    got_core,
    chip_sum,
    got_chip,
    frag_total,
    load_sem,
    store_sem,
    gp1_s, gp1_r, gp2_s, gp2_r, gy_s, gy_r, gq1_s, gq1_r, gq2_s, gq2_r,
    rq1_s, rq1_r, rq2_s, rq2_r, ry_s, ry_r, rp1_s, rp1_r, rp2_s, rp2_r,
    frag_s, frag_r,
):
    f = lax.axis_index("fsdp")
    y, x, z = f // 16, (f // 4) % 4, f % 4
    first_of = (x, z)
    last_of = (z, x)
    rows = w.shape[1] // 32
    half = rows // 2
    kv = w.shape[2]
    kh = kv // 2
    cols = N * rows

    def device(yy, xx, zz):
        return (yy * 4 + xx) * 4 + zz

    def block(t, yy, p, q):
        return device(yy, p, q) if t == 0 else device(yy, q, p)

    def along_first(t, step):
        return block(t, y, (first_of[t] + step) % 4, last_of[t])

    def along_last(t, step):
        return block(t, y, first_of[t], (last_of[t] + step) % 4)

    partner = device(1 - y, x, z)

    def send_to(src, dst, ss, rs, target):
        return pltpu.make_async_remote_copy(
            src_ref=src, dst_ref=dst, send_sem=ss, recv_sem=rs,
            device_id={"fsdp": target}, device_id_type=pl.DeviceIdType.MESH,
        )

    def w_at(t, b, part_of=None):
        if part_of is None:
            return w.at[t, pl.ds(pl.multiple_of(b * rows, rows), rows)]
        return w.at[t, pl.ds(pl.multiple_of(b * rows + part_of * half, half), half)]

    def sign(d):
        return 1 if d == 0 else 3

    def gp1(t, d):
        own = w_at(t, f)
        return send_to(own, own, gp1_s.at[t, d], gp1_r.at[t, d], along_first(t, sign(d)))

    def gp2(t, d):
        ref = w_at(t, along_first(t, 4 - sign(d)), d)
        return send_to(ref, ref, gp2_s.at[t, d], gp2_r.at[t, d], along_first(t, sign(d)))

    def gy(t, k):
        ref = w_at(t, along_first(t, k))
        return send_to(ref, ref, gy_s.at[t, k], gy_r.at[t, k], partner)

    def gather_item(t, i):
        plane = (y + i // 4) % 2
        return plane, (first_of[t] + i) % 4

    def gq1(t, i, d):
        plane, p = gather_item(t, i)
        ref = w_at(t, block(t, plane, p, last_of[t]))
        return send_to(ref, ref, gq1_s.at[t, i, d], gq1_r.at[t, i, d], along_last(t, sign(d)))

    def gq2(t, i, d):
        plane, p = gather_item(t, i)
        ref = w_at(t, block(t, plane, p, (last_of[t] + 4 - sign(d)) % 4), d)
        return send_to(ref, ref, gq2_s.at[t, i, d], gq2_r.at[t, i, d], along_last(t, sign(d)))

    def reduce_item(t, i):
        plane = (y + 1 + i // 4) % 2
        return plane, (first_of[t] + i + 1) % 4

    def part_at(t, i, q, part_of=None):
        ref = part.at[t, i, q]
        return ref if part_of is None else ref.at[pl.ds(part_of * kh, kh)]

    def rq1(t, i, d):
        return send_to(
            part_at(t, i, (last_of[t] + 2) % 4, d), got_a.at[t, i, d],
            rq1_s.at[t, i, d], rq1_r.at[t, i, d], along_last(t, sign(d)),
        )

    def rq2(t, i, d):
        return send_to(
            part_at(t, i, (last_of[t] + sign(d)) % 4), got_b.at[t, i, d],
            rq2_s.at[t, i, d], rq2_r.at[t, i, d], along_last(t, sign(d)),
        )

    def ry(t, k):
        return send_to(
            part_at(t, k, last_of[t]), got_y.at[t, k], ry_s.at[t, k], ry_r.at[t, k], partner
        )

    def rp1(t, d):
        return send_to(
            part_at(t, 5, last_of[t], d), got_pa.at[t, d],
            rp1_s.at[t, d], rp1_r.at[t, d], along_first(t, sign(d)),
        )

    def rp2(t, d):
        return send_to(
            part_at(t, 4 if d == 0 else 6, last_of[t]), got_pb.at[t, d],
            rp2_s.at[t, d], rp2_r.at[t, d], along_first(t, sign(d)),
        )

    rep = lax.axis_index("replica")
    core = rep % 2
    other_core = rep + 1 - 2 * core
    other_chip = rep + 2 - 4 * (rep // 2)

    def frag_copy(k, src, dst, target):
        return pltpu.make_async_remote_copy(
            src_ref=src, dst_ref=dst, send_sem=frag_s.at[k], recv_sem=frag_r.at[k],
            device_id={"replica": target}, device_id_type=pl.DeviceIdType.MESH,
        )

    def frag_core():
        return frag_copy(0, pseudo, got_core, other_core)

    def frag_chip():
        return frag_copy(1, chip_sum, got_chip, other_chip)

    def frag_back():
        return frag_copy(2, frag_total.at[core], frag_total.at[core], other_core)

    types = (0, 1)
    ways = (0, 1)

    load_master = pltpu.make_async_copy(master_hbm.at[0], master, load_sem.at[0])
    load_cot = pltpu.make_async_copy(cot_hbm.at[0], cot, load_sem.at[1])
    plane_cols = act.shape[1] // 2

    def load_act(plane, slot):
        at = pl.ds(pl.multiple_of(plane * plane_cols, plane_cols), plane_cols)
        return pltpu.make_async_copy(act_hbm.at[0, :, at], act.at[:, at], load_sem.at[slot])

    load_master.start()
    load_cot.start()
    load_act(1 - y, 2).start()
    load_act(y, 3).start()
    load_frag = [
        pltpu.make_async_copy(outer_hbm, outer, load_sem.at[4]),
        pltpu.make_async_copy(local_hbm.at[0], local, load_sem.at[5]),
        pltpu.make_async_copy(moment_hbm, moment, load_sem.at[6]),
    ]
    store_frag = [
        pltpu.make_async_copy(outer, new_outer_hbm, store_sem.at[9]),
        pltpu.make_async_copy(moment, new_moment_hbm, store_sem.at[10]),
    ]
    for load in load_frag:
        load.start()

    barrier = pltpu.get_barrier_semaphore()
    around = [along_first(0, 1), along_first(0, 3), along_last(0, 1), along_last(0, 3), partner]
    for other in around:
        pl.semaphore_signal(
            barrier, inc=1, device_id={"fsdp": other}, device_id_type=pl.DeviceIdType.MESH
        )
    for other in (other_core, other_chip):
        pl.semaphore_signal(
            barrier, inc=1, device_id={"replica": other}, device_id_type=pl.DeviceIdType.MESH
        )
    load_master.wait()
    own_rows = pl.ds(pl.multiple_of(f * rows, rows), rows)
    for t in types:
        w[t, own_rows, :] = master[:, t * kv:(t + 1) * kv].astype(BF16)
    pl.semaphore_wait(barrier, len(around) + 2)
    for t in types:
        for d in ways:
            gp1(t, d).start()
    for t in types:
        for d in ways:
            gq1(t, 0, d).start()
        gy(t, 0).start()

    load_cot.wait()
    for t in types:
        cot_t[pl.ds(t * kv, kv), :] = cot[:, t * kv:(t + 1) * kv].T
    for t in types:
        acc[t] = jnp.zeros(acc.shape[1:], F32)
    load_act(1 - y, 2).wait()

    def make_parts(i):
        for t in types:
            plane, p = reduce_item(t, i)
            if t == 0:
                at = pl.multiple_of((plane * 4 + p) * cols, cols)
                right = act[:, pl.ds(at, cols)]
            else:
                right = jnp.concatenate(
                    [
                        act[:, pl.ds(pl.multiple_of(device(plane, q, p) * rows, rows), rows)]
                        for q in range(N)
                    ],
                    axis=1,
                )
            for m in range(2):
                at = m * kh
                prod = jnp.dot(
                    cot_t[pl.ds(t * kv + at, kh), :], right, preferred_element_type=F32
                ).astype(BF16)
                for q in range(N):
                    part[t, i, q, pl.ds(at, kh), :] = prod[:, q * rows:(q + 1) * rows]

    def add_half(t, i, d, got):
        at = pl.ds(d * kh, kh)
        q = (last_of[t] + sign(d)) % 4
        total = part[t, i, q, at, :].astype(F32) + got[...].astype(F32)
        part[t, i, q, at, :] = total.astype(BF16)

    def project(i):
        for t in types:
            plane, p = gather_item(t, i)
            if t == 0:
                at = pl.multiple_of((plane * 4 + p) * cols, cols)
                left = act[:, pl.ds(at, cols)]
                right = w[t, pl.ds(at, cols), :]
            else:
                spans = [
                    pl.ds(pl.multiple_of(device(plane, q, p) * rows, rows), rows) for q in range(N)
                ]
                left = jnp.concatenate([act[:, s] for s in spans], axis=1)
                right = jnp.concatenate([w[t, s, :] for s in spans], axis=0)
            acc[t] += jnp.dot(left, right, preferred_element_type=F32)

    def store_igrad(b):
        at = pl.ds(pl.multiple_of(b * cols, cols), cols)
        return pltpu.make_async_copy(igrad.at[:, at], igrad_hbm.at[0, :, at], store_sem.at[b])

    def input_grads(plane):
        def one(k, carry):
            b = plane * 4 + k
            at = pl.ds(pl.multiple_of(b * cols, cols), cols)
            total = None
            for t in types:
                term = lax.dot_general(
                    cot[:, t * kv:(t + 1) * kv], w[t, at, :], (((1,), (1,)), ((), ())),
                    preferred_element_type=F32,
                )
                total = term if total is None else total + term
            igrad[:, at] = total.astype(BF16)
            store_igrad(b).start()
            return carry

        lax.fori_loop(0, N, one, 0)

    def fragment_rounds(r):
        @pl.when(r == 1)
        def _():
            for load in load_frag:
                load.wait()
            pseudo[...] = (outer[1 - core] - local[1 - core]).astype(BF16)
            frag_core().start()

        @pl.when(r == 2)
        def _():
            frag_core().wait_recv()
            summed = outer[core] - local[core] + got_core[...].astype(F32)
            chip_sum[...] = summed.astype(BF16)
            frag_chip().start()

        @pl.when(r == 5)
        def _():
            frag_chip().wait_recv()
            frag_total[core] = chip_sum[...].astype(F32) + got_chip[...].astype(F32)
            frag_back().start()

        @pl.when(r == 6)
        def _():
            frag_back().wait_recv()
            for layer in range(2):
                mean = frag_total[layer] * (1.0 / N_REPLICA)
                new_moment = NESTEROV * moment[layer] + mean
                moment[layer] = new_moment
                outer[layer] = outer[layer] - OUTER_RATE * (mean + NESTEROV * new_moment)
            for store in store_frag:
                store.start()

    def round_of(r, carry):
        @pl.when(r == 1)
        def _():
            for t in types:
                for d in (1, 0):
                    gp1(t, d).wait_recv()
                    gp2(t, d).start()
                gy(t, 1).start()
                gy(t, 3).start()

        @pl.when(r == 2)
        def _():
            for t in types:
                for d in ways:
                    gp2(t, d).wait_recv()
                gy(t, 2).start()

        @pl.when((r >= 4) & (r < ITEMS))
        def _():
            for t in types:
                gy(t, r % 4).wait_recv()

        @pl.when((r >= 1) & (r < ITEMS))
        def _():
            for t in types:
                for d in ways:
                    gq1(t, r, d).start()

        @pl.when(r == LAG_G)
        def _():
            load_act(y, 3).wait()

        @pl.when(r < ITEMS)
        def _():
            make_parts(r)
            for t in types:
                for d in ways:
                    rq1(t, r, d).start()

        fragment_rounds(r)

        @pl.when((r >= LAG_RQ2) & (r < ITEMS + LAG_RQ2))
        def _():
            i = r - LAG_RQ2
            for t in types:
                for d in ways:
                    rq1(t, i, d).wait_recv()
                    add_half(t, i, d, got_a.at[t, i, d])
                    rq2(t, i, d).start()

        @pl.when((r >= LAG_GQ2) & (r < ITEMS + LAG_GQ2))
        def _():
            i = r - LAG_GQ2
            for t in types:
                for d in ways:
                    gq1(t, i, d).wait_recv()
                    gq2(t, i, d).start()

        @pl.when((r >= LAG_RS) & (r < ITEMS + LAG_RS))
        def _():
            i = r - LAG_RS
            for t in types:
                for d in ways:
                    rq2(t, i, d).wait_recv()
                q = last_of[t]
                mine[t] = (
                    part[t, i, q].astype(F32)
                    + got_b[t, i, 0].astype(F32)
                    + got_b[t, i, 1].astype(F32)
                )

                @pl.when(i < 4)
                def _():
                    part[t, i, q] = mine[t].astype(BF16)
                    ry(t, i).start()

                @pl.when(i >= 4)
                def _():
                    ry(t, i % 4).wait_recv()
                    mine[t] += got_y[t, i % 4].astype(F32)

                @pl.when((i >= 4) & (i < 7))
                def _():
                    part[t, i, q] = mine[t].astype(BF16)

            @pl.when(i == 5)
            def _():
                for t in types:
                    for d in ways:
                        rp1(t, d).start()

            @pl.when(i == 6)
            def _():
                for t in types:
                    for d in ways:
                        rp1(t, d).wait_recv()
                        at = pl.ds(d * kh, kh)
                        k = 4 if d == 0 else 6
                        total = part[t, k, last_of[t], at, :].astype(F32)
                        total += got_pa[t, d].astype(F32)
                        part[t, k, last_of[t], at, :] = total.astype(BF16)
                        rp2(t, d).start()

        @pl.when((r >= LAG_G) & (r < ITEMS + LAG_G))
        def _():
            i = r - LAG_G
            for t in types:
                for d in ways:
                    gq2(t, i, d).wait_recv()
            project(i)

            @pl.when(i == 3)
            def _():
                input_grads(y)

            @pl.when(i == 7)
            def _():
                input_grads(1 - y)

        return carry

    lax.fori_loop(0, ROUNDS, round_of, 0)

    for t in types:
        out[:, t * kv:(t + 1) * kv] = acc[t].astype(BF16)
    store_out = pltpu.make_async_copy(out, out_hbm.at[0], store_sem.at[8])
    store_out.start()
    for t in types:
        for d in ways:
            rp2(t, d).wait_recv()
        total = mine[t] + got_pb[t, 0].astype(F32) + got_pb[t, 1].astype(F32)
        grad_ref[:, t * kv:(t + 1) * kv] = total.T

    for t in types:
        for d in ways:
            gp1(t, d).wait_send()
            gp2(t, d).wait_send()
            rp1(t, d).wait_send()
            rp2(t, d).wait_send()

    def drain_four(k, carry):
        for t in types:
            gy(t, k).wait_send()
            ry(t, k).wait_send()
        return carry

    def drain_eight(i, carry):
        for t in types:
            for d in ways:
                gq1(t, i, d).wait_send()
                gq2(t, i, d).wait_send()
                rq1(t, i, d).wait_send()
                rq2(t, i, d).wait_send()
        store_igrad(i).wait()
        return carry

    for copy in (frag_core(), frag_chip(), frag_back()):
        copy.wait_send()
    for store in store_frag:
        store.wait()
    lax.fori_loop(0, N, drain_four, 0)
    lax.fori_loop(0, ITEMS, drain_eight, 0)
    store_out.wait()


def train_step(activations, cotangent, master, outer, local, moment):
    tok, width = activations.shape[1:]
    kv2 = cotangent.shape[2]
    rows = master.shape[1]
    kv, kh = kv2 // 2, kv2 // 4
    dma = pltpu.SemaphoreType.DMA
    sems = []
    for shape in ((2, 2), (2, 2), (2, 4), (2, 8, 2), (2, 8, 2)):
        sems += [dma(shape), dma(shape)]
    for shape in ((2, 8, 2), (2, 8, 2), (2, 4), (2, 2), (2, 2)):
        sems += [dma(shape), dma(shape)]
    sems += [dma((3,)), dma((3,))]
    layer = outer.shape[1:]
    hbm = pl.BlockSpec(memory_space=pl.ANY)
    return pl.pallas_call(
        train_kernel,
        out_shape=(
            jax.ShapeDtypeStruct((1, tok, kv2), BF16),
            jax.ShapeDtypeStruct((1, tok, width), BF16),
            jax.ShapeDtypeStruct((rows, kv2), F32),
            jax.ShapeDtypeStruct(outer.shape, F32),
            jax.ShapeDtypeStruct(outer.shape, F32),
        ),
        in_specs=[hbm] * 6,
        out_specs=(hbm, hbm, pl.BlockSpec(memory_space=pltpu.VMEM), hbm, hbm),
        scratch_shapes=[
            pltpu.VMEM((tok, width), BF16),
            pltpu.VMEM((tok, kv2), BF16),
            pltpu.VMEM((kv2, tok), BF16),
            pltpu.VMEM((rows, kv2), F32),
            pltpu.VMEM((2, width, kv), BF16),
            pltpu.VMEM((2, 8, 4, kv, rows), BF16),
            pltpu.VMEM((2, 8, 2, kh, rows), BF16),
            pltpu.VMEM((2, 8, 2, kv, rows), BF16),
            pltpu.VMEM((2, 4, kv, rows), BF16),
            pltpu.VMEM((2, 2, kh, rows), BF16),
            pltpu.VMEM((2, 2, kv, rows), BF16),
            pltpu.VMEM((2, kv, rows), F32),
            pltpu.VMEM((2, tok, kv), F32),
            pltpu.VMEM((tok, kv2), BF16),
            pltpu.VMEM((tok, width), BF16),
            pltpu.VMEM((2, *layer), F32),
            pltpu.VMEM((2, *layer), F32),
            pltpu.VMEM((2, *layer), F32),
            pltpu.VMEM(layer, BF16),
            pltpu.VMEM(layer, BF16),
            pltpu.VMEM(layer, BF16),
            pltpu.VMEM(layer, BF16),
            pltpu.VMEM((2, *layer), F32),
            dma((7,)),
            dma((11,)),
            *sems,
        ],
        compiler_params=pltpu.CompilerParams(
            collective_id=0, has_side_effects=True, vmem_limit_bytes=56 * 2**20
        ),
        cost_estimate=pl.CostEstimate(
            flops=6 * tok * width * kv2, bytes_accessed=100 * 2**20, transcendentals=0
        ),
        name="train_step",
    )(activations, cotangent, master, outer, local, moment)


def shards(
    activations,
    kv_cotangent,
    kv_master,
    kv_first,
    kv_second,
    outer_params,
    local_params,
    outer_momentum,
):
    projected, input_grad, summed, new_outer, new_momentum = train_step(
        activations, kv_cotangent, kv_master, outer_params, local_params, outer_momentum
    )
    all_tokens = activations.shape[1] * lax.axis_size("fsdp")
    grad = summed * (1.0 / math.sqrt(all_tokens))
    new_master, new_first, new_second = adam_update(
        kv_master[0], kv_first[0], kv_second[0], grad
    )

    return (
        projected,
        input_grad,
        new_master[None],
        new_first[None],
        new_second[None],
        new_outer,
        new_momentum,
    )


def solution(mesh):
    row_split = P("replica", "fsdp", None)
    fragment = P(None, "fsdp", None)
    return jax.shard_map(
        shards,
        mesh=mesh,
        in_specs=(
            row_split,
            row_split,
            row_split,
            row_split,
            row_split,
            fragment,
            P("replica", None, "fsdp", None),
            fragment,
        ),
        out_specs=(row_split, row_split, row_split, row_split, row_split, fragment, fragment),
        check_vma=False,
    )
```

```python
import math

import jax
import jax.numpy as jnp
from jax import lax
from jax.experimental import pallas as pl
from jax.experimental.pallas import tpu as pltpu
from jax.sharding import PartitionSpec as P

FIRST_DECAY = 0.9
SECOND_DECAY = 0.95
ADAM_STEPS = 20.0
ADAM_EPSILON = 1e-08
INNER_RATE = 0.01
WEIGHT_DECAY = 0.1
NESTEROV = 0.9
OUTER_RATE = 0.7

BF16 = jnp.bfloat16
F32 = jnp.float32
N_REPLICA = 4
N = 4
ITEMS = 2 * N
LAG_RQ2 = 1
LAG_RS = 2
LAG_GQ2 = 1
LAG_G = 2
ROUNDS = ITEMS + 2


def adam_update(master, first, second, grad):
    first = FIRST_DECAY * first + (1.0 - FIRST_DECAY) * grad
    second = SECOND_DECAY * second + (1.0 - SECOND_DECAY) * grad * grad
    first_fix = 1.0 - FIRST_DECAY**ADAM_STEPS
    second_fix = 1.0 - SECOND_DECAY**ADAM_STEPS
    update = first / first_fix / (jnp.sqrt(second / second_fix) + ADAM_EPSILON)
    master = master - INNER_RATE * (update + WEIGHT_DECAY * master)
    return (master, first, second)


def train_kernel(
    act_hbm,
    cot_hbm,
    master_hbm,
    outer_hbm,
    local_hbm,
    moment_hbm,
    first_hbm,
    second_hbm,
    out,
    igrad,
    master,
    first,
    second,
    outer,
    moment,
    act,
    cot,
    cot_t,
    w,
    part,
    got_a,
    got_b,
    got_y,
    got_pa,
    got_pb,
    mine,
    acc,
    local,
    pseudo,
    got_core,
    chip_sum,
    got_chip,
    frag_total,
    load_sem,
    gp1_s, gp1_r, gp2_s, gp2_r, gy_s, gy_r, gq1_s, gq1_r, gq2_s, gq2_r,
    rq1_s, rq1_r, rq2_s, rq2_r, ry_s, ry_r, rp1_s, rp1_r, rp2_s, rp2_r,
    frag_s, frag_r,
):
    f = lax.axis_index("fsdp")
    y, x, z = f // 16, (f // 4) % 4, f % 4
    first_of = (x, z)
    last_of = (z, x)
    rows = w.shape[1] // 32
    half = rows // 2
    kv = w.shape[2]
    kh = kv // 2
    cols = N * rows

    def device(yy, xx, zz):
        return (yy * 4 + xx) * 4 + zz

    def block(t, yy, p, q):
        return device(yy, p, q) if t == 0 else device(yy, q, p)

    def along_first(t, step):
        return block(t, y, (first_of[t] + step) % 4, last_of[t])

    def along_last(t, step):
        return block(t, y, first_of[t], (last_of[t] + step) % 4)

    partner = device(1 - y, x, z)

    def send_to(src, dst, ss, rs, target):
        return pltpu.make_async_remote_copy(
            src_ref=src, dst_ref=dst, send_sem=ss, recv_sem=rs,
            device_id={"fsdp": target}, device_id_type=pl.DeviceIdType.MESH,
        )

    def w_at(t, b, part_of=None):
        if part_of is None:
            return w.at[t, pl.ds(pl.multiple_of(b * rows, rows), rows)]
        return w.at[t, pl.ds(pl.multiple_of(b * rows + part_of * half, half), half)]

    def sign(d):
        return 1 if d == 0 else 3

    def gp1(t, d):
        own = w_at(t, f)
        return send_to(own, own, gp1_s.at[t, d], gp1_r.at[t, d], along_first(t, sign(d)))

    def gp2(t, d):
        ref = w_at(t, along_first(t, 4 - sign(d)), d)
        return send_to(ref, ref, gp2_s.at[t, d], gp2_r.at[t, d], along_first(t, sign(d)))

    def gy(t, k):
        ref = w_at(t, along_first(t, k))
        return send_to(ref, ref, gy_s.at[t, k], gy_r.at[t, k], partner)

    def gather_item(t, i):
        plane = (y + i // 4) % 2
        return plane, (first_of[t] + i) % 4

    def gq1(t, i, d):
        plane, p = gather_item(t, i)
        ref = w_at(t, block(t, plane, p, last_of[t]))
        return send_to(ref, ref, gq1_s.at[t, i, d], gq1_r.at[t, i, d], along_last(t, sign(d)))

    def gq2(t, i, d):
        plane, p = gather_item(t, i)
        ref = w_at(t, block(t, plane, p, (last_of[t] + 4 - sign(d)) % 4), d)
        return send_to(ref, ref, gq2_s.at[t, i, d], gq2_r.at[t, i, d], along_last(t, sign(d)))

    def reduce_item(t, i):
        plane = (y + 1 + i // 4) % 2
        return plane, (first_of[t] + i + 1) % 4

    def part_at(t, i, q, part_of=None):
        ref = part.at[t, i, q]
        return ref if part_of is None else ref.at[pl.ds(part_of * kh, kh)]

    def rq1(t, i, d):
        return send_to(
            part_at(t, i, (last_of[t] + 2) % 4, d), got_a.at[t, i, d],
            rq1_s.at[t, i, d], rq1_r.at[t, i, d], along_last(t, sign(d)),
        )

    def rq2(t, i, d):
        return send_to(
            part_at(t, i, (last_of[t] + sign(d)) % 4), got_b.at[t, i, d],
            rq2_s.at[t, i, d], rq2_r.at[t, i, d], along_last(t, sign(d)),
        )

    def ry(t, k):
        return send_to(
            part_at(t, k, last_of[t]), got_y.at[t, k], ry_s.at[t, k], ry_r.at[t, k], partner
        )

    def rp1(t, d):
        return send_to(
            part_at(t, 5, last_of[t], d), got_pa.at[t, d],
            rp1_s.at[t, d], rp1_r.at[t, d], along_first(t, sign(d)),
        )

    def rp2(t, d):
        return send_to(
            part_at(t, 4 if d == 0 else 6, last_of[t]), got_pb.at[t, d],
            rp2_s.at[t, d], rp2_r.at[t, d], along_first(t, sign(d)),
        )

    rep = lax.axis_index("replica")
    core = rep % 2
    other_core = rep + 1 - 2 * core
    other_chip = rep + 2 - 4 * (rep // 2)

    def frag_copy(k, src, dst, target):
        return pltpu.make_async_remote_copy(
            src_ref=src, dst_ref=dst, send_sem=frag_s.at[k], recv_sem=frag_r.at[k],
            device_id={"replica": target}, device_id_type=pl.DeviceIdType.MESH,
        )

    def frag_core():
        return frag_copy(0, pseudo, got_core, other_core)

    def frag_chip():
        return frag_copy(1, chip_sum, got_chip, other_chip)

    def frag_back():
        return frag_copy(2, frag_total.at[core], frag_total.at[core], other_core)

    types = (0, 1)
    ways = (0, 1)

    load_master = pltpu.make_async_copy(master_hbm, master, load_sem.at[0])
    load_cot = pltpu.make_async_copy(cot_hbm.at[0], cot, load_sem.at[1])
    plane_cols = act.shape[1] // 2

    def load_act(plane, slot):
        at = pl.ds(pl.multiple_of(plane * plane_cols, plane_cols), plane_cols)
        return pltpu.make_async_copy(act_hbm.at[0, :, at], act.at[:, at], load_sem.at[slot])

    load_master.start()
    load_cot.start()
    load_act(1 - y, 2).start()
    load_act(y, 3).start()
    load_frag = [
        pltpu.make_async_copy(outer_hbm, outer, load_sem.at[4]),
        pltpu.make_async_copy(local_hbm.at[0], local, load_sem.at[5]),
        pltpu.make_async_copy(moment_hbm, moment, load_sem.at[6]),
    ]
    load_adam = [
        pltpu.make_async_copy(first_hbm, first, load_sem.at[7]),
        pltpu.make_async_copy(second_hbm, second, load_sem.at[8]),
    ]
    for load in load_adam:
        load.start()
    for load in load_frag:
        load.start()

    barrier = pltpu.get_barrier_semaphore()
    around = [along_first(0, 1), along_first(0, 3), along_last(0, 1), along_last(0, 3), partner]
    for other in around:
        pl.semaphore_signal(
            barrier, inc=1, device_id={"fsdp": other}, device_id_type=pl.DeviceIdType.MESH
        )
    for other in (other_core, other_chip):
        pl.semaphore_signal(
            barrier, inc=1, device_id={"replica": other}, device_id_type=pl.DeviceIdType.MESH
        )
    load_master.wait()
    own_rows = pl.ds(pl.multiple_of(f * rows, rows), rows)
    for t in types:
        w[t, own_rows, :] = master[0, :, t * kv:(t + 1) * kv].astype(BF16)
    pl.semaphore_wait(barrier, len(around) + 2)
    for t in types:
        for d in ways:
            gp1(t, d).start()
    for t in types:
        for d in ways:
            gq1(t, 0, d).start()
        gy(t, 0).start()

    load_cot.wait()
    for t in types:
        cot_t[pl.ds(t * kv, kv), :] = cot[:, t * kv:(t + 1) * kv].T
    for t in types:
        acc[t] = jnp.zeros(acc.shape[1:], F32)
    load_act(1 - y, 2).wait()

    def make_parts(i):
        for t in types:
            plane, p = reduce_item(t, i)
            if t == 0:
                at = pl.multiple_of((plane * 4 + p) * cols, cols)
                right = act[:, pl.ds(at, cols)]
            else:
                right = jnp.concatenate(
                    [
                        act[:, pl.ds(pl.multiple_of(device(plane, q, p) * rows, rows), rows)]
                        for q in range(N)
                    ],
                    axis=1,
                )
            for m in range(2):
                at = m * kh
                prod = jnp.dot(
                    cot_t[pl.ds(t * kv + at, kh), :], right, preferred_element_type=F32
                ).astype(BF16)
                for q in range(N):
                    part[t, i, q, pl.ds(at, kh), :] = prod[:, q * rows:(q + 1) * rows]

    def add_half(t, i, d, got):
        at = pl.ds(d * kh, kh)
        q = (last_of[t] + sign(d)) % 4
        total = part[t, i, q, at, :].astype(F32) + got[...].astype(F32)
        part[t, i, q, at, :] = total.astype(BF16)

    def project(i):
        for t in types:
            plane, p = gather_item(t, i)
            if t == 0:
                at = pl.multiple_of((plane * 4 + p) * cols, cols)
                left = act[:, pl.ds(at, cols)]
                right = w[t, pl.ds(at, cols), :]
            else:
                spans = [
                    pl.ds(pl.multiple_of(device(plane, q, p) * rows, rows), rows) for q in range(N)
                ]
                left = jnp.concatenate([act[:, s] for s in spans], axis=1)
                right = jnp.concatenate([w[t, s, :] for s in spans], axis=0)
            acc[t] += jnp.dot(left, right, preferred_element_type=F32)

    def input_grads(plane):
        def one(k, carry):
            b = plane * 4 + k
            at = pl.ds(pl.multiple_of(b * cols, cols), cols)
            total = None
            for t in types:
                term = lax.dot_general(
                    cot[:, t * kv:(t + 1) * kv], w[t, at, :], (((1,), (1,)), ((), ())),
                    preferred_element_type=F32,
                )
                total = term if total is None else total + term
            igrad[0, :, at] = total.astype(BF16)
            return carry

        lax.fori_loop(0, N, one, 0)

    def fragment_rounds(r):
        @pl.when(r == 1)
        def _():
            for load in load_frag:
                load.wait()
            pseudo[...] = (outer[1 - core] - local[1 - core]).astype(BF16)
            frag_core().start()

        @pl.when(r == 2)
        def _():
            frag_core().wait_recv()
            summed = outer[core] - local[core] + got_core[...].astype(F32)
            chip_sum[...] = summed.astype(BF16)
            frag_chip().start()

        @pl.when(r == 5)
        def _():
            frag_chip().wait_recv()
            frag_total[core] = chip_sum[...].astype(F32) + got_chip[...].astype(F32)
            frag_back().start()

        @pl.when(r == 6)
        def _():
            frag_back().wait_recv()
            for layer in range(2):
                mean = frag_total[layer] * (1.0 / N_REPLICA)
                new_moment = NESTEROV * moment[layer] + mean
                moment[layer] = new_moment
                outer[layer] = outer[layer] - OUTER_RATE * (mean + NESTEROV * new_moment)

    def round_of(r, carry):
        @pl.when(r == 1)
        def _():
            for t in types:
                for d in (1, 0):
                    gp1(t, d).wait_recv()
                    gp2(t, d).start()
                gy(t, 1).start()
                gy(t, 3).start()

        @pl.when(r == 2)
        def _():
            for t in types:
                for d in ways:
                    gp2(t, d).wait_recv()
                gy(t, 2).start()

        @pl.when((r >= 4) & (r < ITEMS))
        def _():
            for t in types:
                gy(t, r % 4).wait_recv()

        @pl.when((r >= 1) & (r < ITEMS))
        def _():
            for t in types:
                for d in ways:
                    gq1(t, r, d).start()

        @pl.when(r == LAG_G)
        def _():
            load_act(y, 3).wait()

        @pl.when(r < ITEMS)
        def _():
            make_parts(r)
            for t in types:
                for d in ways:
                    rq1(t, r, d).start()

        fragment_rounds(r)

        @pl.when((r >= LAG_RQ2) & (r < ITEMS + LAG_RQ2))
        def _():
            i = r - LAG_RQ2
            for t in types:
                for d in ways:
                    rq1(t, i, d).wait_recv()
                    add_half(t, i, d, got_a.at[t, i, d])
                    rq2(t, i, d).start()

        @pl.when((r >= LAG_GQ2) & (r < ITEMS + LAG_GQ2))
        def _():
            i = r - LAG_GQ2
            for t in types:
                for d in ways:
                    gq1(t, i, d).wait_recv()
                    gq2(t, i, d).start()

        @pl.when((r >= LAG_RS) & (r < ITEMS + LAG_RS))
        def _():
            i = r - LAG_RS
            for t in types:
                for d in ways:
                    rq2(t, i, d).wait_recv()
                q = last_of[t]
                mine[t] = (
                    part[t, i, q].astype(F32)
                    + got_b[t, i, 0].astype(F32)
                    + got_b[t, i, 1].astype(F32)
                )

                @pl.when(i < 4)
                def _():
                    part[t, i, q] = mine[t].astype(BF16)
                    ry(t, i).start()

                @pl.when(i >= 4)
                def _():
                    ry(t, i % 4).wait_recv()
                    mine[t] += got_y[t, i % 4].astype(F32)

                @pl.when((i >= 4) & (i < 7))
                def _():
                    part[t, i, q] = mine[t].astype(BF16)

            @pl.when(i == 5)
            def _():
                for t in types:
                    for d in ways:
                        rp1(t, d).start()

            @pl.when(i == 6)
            def _():
                for t in types:
                    for d in ways:
                        rp1(t, d).wait_recv()
                        at = pl.ds(d * kh, kh)
                        k = 4 if d == 0 else 6
                        total = part[t, k, last_of[t], at, :].astype(F32)
                        total += got_pa[t, d].astype(F32)
                        part[t, k, last_of[t], at, :] = total.astype(BF16)
                        rp2(t, d).start()

        @pl.when((r >= LAG_G) & (r < ITEMS + LAG_G))
        def _():
            i = r - LAG_G
            for t in types:
                for d in ways:
                    gq2(t, i, d).wait_recv()
            project(i)

            @pl.when(i == 3)
            def _():
                input_grads(y)

            @pl.when(i == 7)
            def _():
                input_grads(1 - y)

        return carry

    lax.fori_loop(0, ROUNDS, round_of, 0)

    for t in types:
        out[0, :, t * kv:(t + 1) * kv] = acc[t].astype(BF16)
    for load in load_adam:
        load.wait()
    tokens = act.shape[0] * 32
    for t in types:
        for d in ways:
            rp2(t, d).wait_recv()
        total = mine[t] + got_pb[t, 0].astype(F32) + got_pb[t, 1].astype(F32)
        at = pl.ds(t * kv, kv)
        master[0, :, at], first[0, :, at], second[0, :, at] = adam_update(
            master[0, :, at], first[0, :, at], second[0, :, at],
            total.T * (1.0 / math.sqrt(tokens)),
        )

    for t in types:
        for d in ways:
            gp1(t, d).wait_send()
            gp2(t, d).wait_send()
            rp1(t, d).wait_send()
            rp2(t, d).wait_send()

    def drain_four(k, carry):
        for t in types:
            gy(t, k).wait_send()
            ry(t, k).wait_send()
        return carry

    def drain_eight(i, carry):
        for t in types:
            for d in ways:
                gq1(t, i, d).wait_send()
                gq2(t, i, d).wait_send()
                rq1(t, i, d).wait_send()
                rq2(t, i, d).wait_send()
        return carry

    for copy in (frag_core(), frag_chip(), frag_back()):
        copy.wait_send()
    lax.fori_loop(0, N, drain_four, 0)
    lax.fori_loop(0, ITEMS, drain_eight, 0)


def write_kernel(*refs):
    count = len(refs) // 2
    sem = refs[-1]
    copies = [
        pltpu.make_async_copy(refs[k], refs[count + k], sem.at[k]) for k in range(count)
    ]
    for copy in copies:
        copy.start()
    for copy in copies:
        copy.wait()


def write_out(results):
    return pl.pallas_call(
        write_kernel,
        out_shape=tuple(jax.ShapeDtypeStruct(r.shape, r.dtype) for r in results),
        in_specs=[pl.BlockSpec(memory_space=pltpu.VMEM)] * len(results),
        out_specs=tuple(pl.BlockSpec(memory_space=pl.ANY) for _ in results),
        scratch_shapes=[pltpu.SemaphoreType.DMA((len(results),))],
        compiler_params=pltpu.CompilerParams(vmem_limit_bytes=16 * 2**20),
        name="write_out",
    )(*results)


def train_step(activations, cotangent, master, outer, local, moment, first, second):
    tok, width = activations.shape[1:]
    kv2 = cotangent.shape[2]
    rows = master.shape[1]
    kv, kh = kv2 // 2, kv2 // 4
    dma = pltpu.SemaphoreType.DMA
    sems = []
    for shape in ((2, 2), (2, 2), (2, 4), (2, 8, 2), (2, 8, 2)):
        sems += [dma(shape), dma(shape)]
    for shape in ((2, 8, 2), (2, 8, 2), (2, 4), (2, 2), (2, 2)):
        sems += [dma(shape), dma(shape)]
    sems += [dma((3,)), dma((3,))]
    layer = outer.shape[1:]
    hbm = pl.BlockSpec(memory_space=pl.ANY)
    return pl.pallas_call(
        train_kernel,
        out_shape=(
            pltpu.VMEM((1, tok, kv2), BF16),
            pltpu.VMEM((1, tok, width), BF16),
            pltpu.VMEM((1, rows, kv2), F32),
            pltpu.VMEM((1, rows, kv2), F32),
            pltpu.VMEM((1, rows, kv2), F32),
            pltpu.VMEM(outer.shape, F32),
            pltpu.VMEM(outer.shape, F32),
        ),
        in_specs=[hbm] * 8,
        out_specs=tuple(pl.BlockSpec(memory_space=pltpu.VMEM) for _ in range(7)),
        scratch_shapes=[
            pltpu.VMEM((tok, width), BF16),
            pltpu.VMEM((tok, kv2), BF16),
            pltpu.VMEM((kv2, tok), BF16),
            pltpu.VMEM((2, width, kv), BF16),
            pltpu.VMEM((2, 8, 4, kv, rows), BF16),
            pltpu.VMEM((2, 8, 2, kh, rows), BF16),
            pltpu.VMEM((2, 8, 2, kv, rows), BF16),
            pltpu.VMEM((2, 4, kv, rows), BF16),
            pltpu.VMEM((2, 2, kh, rows), BF16),
            pltpu.VMEM((2, 2, kv, rows), BF16),
            pltpu.VMEM((2, kv, rows), F32),
            pltpu.VMEM((2, tok, kv), F32),
            pltpu.VMEM((2, *layer), F32),
            pltpu.VMEM(layer, BF16),
            pltpu.VMEM(layer, BF16),
            pltpu.VMEM(layer, BF16),
            pltpu.VMEM(layer, BF16),
            pltpu.VMEM((2, *layer), F32),
            dma((9,)),
            *sems,
        ],
        compiler_params=pltpu.CompilerParams(
            collective_id=0, has_side_effects=True, vmem_limit_bytes=46 * 2**20
        ),
        cost_estimate=pl.CostEstimate(
            flops=6 * tok * width * kv2, bytes_accessed=100 * 2**20, transcendentals=0
        ),
        name="train_step",
    )(activations, cotangent, master, outer, local, moment, first, second)


def shards(
    activations,
    kv_cotangent,
    kv_master,
    kv_first,
    kv_second,
    outer_params,
    local_params,
    outer_momentum,
):
    return write_out(
        train_step(
            activations, kv_cotangent, kv_master, outer_params, local_params, outer_momentum,
            kv_first, kv_second,
        )
    )


def solution(mesh):
    row_split = P("replica", "fsdp", None)
    fragment = P(None, "fsdp", None)
    return jax.shard_map(
        shards,
        mesh=mesh,
        in_specs=(
            row_split,
            row_split,
            row_split,
            row_split,
            row_split,
            fragment,
            P("replica", None, "fsdp", None),
            fragment,
        ),
        out_specs=(row_split, row_split, row_split, row_split, row_split, fragment, fragment),
        check_vma=False,
    )
```

```python
import functools
import math

import jax
import jax.numpy as jnp
from jax import lax
from jax.experimental import pallas as pl
from jax.experimental.pallas import tpu as pltpu
from jax.sharding import PartitionSpec as P

FIRST_DECAY = 0.9
SECOND_DECAY = 0.95
ADAM_STEPS = 20.0
ADAM_EPSILON = 1e-08
INNER_RATE = 0.01
WEIGHT_DECAY = 0.1
NESTEROV = 0.9
OUTER_RATE = 0.7

BF16 = jnp.bfloat16
F32 = jnp.float32
N_REPLICA = 4
N = 4
ITEMS = 2 * N
LAG_RQ2 = 1
LAG_RS = 2
LAG_GQ2 = 1
LAG_G = 2
ROUNDS = ITEMS + 2
GATHER_LATE = 16
REDUCE_EARLY = 64


def adam_update(master, first, second, grad):
    first = FIRST_DECAY * first + (1.0 - FIRST_DECAY) * grad
    second = SECOND_DECAY * second + (1.0 - SECOND_DECAY) * grad * grad
    first_fix = 1.0 - FIRST_DECAY**ADAM_STEPS
    second_fix = 1.0 - SECOND_DECAY**ADAM_STEPS
    update = first / first_fix / (jnp.sqrt(second / second_fix) + ADAM_EPSILON)
    master = master - INNER_RATE * (update + WEIGHT_DECAY * master)
    return (master, first, second)


def train_kernel(
    act_hbm,
    cot_hbm,
    master_hbm,
    outer_hbm,
    local_hbm,
    moment_hbm,
    first_hbm,
    second_hbm,
    out,
    igrad,
    master,
    first,
    second,
    outer,
    moment,
    act,
    cot,
    cot_t,
    w,
    part,
    got_a,
    got_b,
    got_l,
    got_y,
    got_pa,
    got_pb,
    mine,
    acc,
    local,
    pseudo,
    got_core,
    chip_sum,
    got_chip,
    frag_total,
    load_sem,
    gp1_s, gp1_r, gp2_s, gp2_r, gy_s, gy_r, gq1_s, gq1_r, gq2_s, gq2_r,
    rq1_s, rq1_r, rq2_s, rq2_r, ry_s, ry_r, rp1_s, rp1_r, rp2_s, rp2_r,
    frag_s, frag_r, gl_s, gl_r, rl_s, rl_r,
):
    f = lax.axis_index("fsdp")
    y, x, z = f // 16, (f // 4) % 4, f % 4
    first_of = (x, z)
    last_of = (z, x)
    rows, kv = w.shape[4:]
    half = rows // 2
    cols = N * rows
    keep_g = rows - GATHER_LATE
    keep_r = kv - REDUCE_EARLY

    def device(yy, xx, zz):
        return (yy * 4 + xx) * 4 + zz

    def along_first(t, step):
        p = (first_of[t] + step) % 4
        return device(y, p, z) if t == 0 else device(y, x, p)

    def along_last(t, step):
        q = (last_of[t] + step) % 4
        return device(y, x, q) if t == 0 else device(y, q, z)

    partner = device(1 - y, x, z)

    def send_to(src, dst, ss, rs, target):
        return pltpu.make_async_remote_copy(
            src_ref=src, dst_ref=dst, send_sem=ss, recv_sem=rs,
            device_id={"fsdp": target}, device_id_type=pl.DeviceIdType.MESH,
        )

    def w_at(t, plane, p, q, start=0, stop=rows):
        a, b = (p, q) if t == 0 else (q, p)
        return w.at[t, plane, a, b, pl.ds(start, stop - start)]

    def sign(d):
        return 1 if d == 0 else 3

    def gp1(t, d):
        own = w_at(t, y, first_of[t], last_of[t])
        return send_to(own, own, gp1_s.at[t, d], gp1_r.at[t, d], along_first(t, sign(d)))

    def gp2(t, d):
        ref = w_at(t, y, (first_of[t] + 4 - sign(d)) % 4, last_of[t], d * half, d * half + half)
        return send_to(ref, ref, gp2_s.at[t, d], gp2_r.at[t, d], along_first(t, sign(d)))

    def gy(t, k):
        ref = w_at(t, y, (first_of[t] + k) % 4, last_of[t], 0, keep_g)
        return send_to(ref, ref, gy_s.at[t, k], gy_r.at[t, k], partner)

    def gather_item(t, i):
        plane = (y + i // 4) % 2
        return plane, (first_of[t] + i) % 4

    def gl(t, k):
        p = (first_of[t] + k) % 4
        late = pl.ds(keep_g, GATHER_LATE)
        ref = w.at[0, y, p, :, late] if t == 0 else w.at[1, y, :, p, late]
        return send_to(ref, ref, gl_s.at[t, k], gl_r.at[t, k], partner)

    def gq1(t, i, d, far):
        plane, p = gather_item(t, i)
        ref = w_at(t, plane, p, last_of[t], 0, keep_g if far else rows)
        return send_to(ref, ref, gq1_s.at[t, i, d], gq1_r.at[t, i, d], along_last(t, sign(d)))

    def gq2(t, i, d, far):
        plane, p = gather_item(t, i)
        end = keep_g if far else rows
        q = (last_of[t] + 4 - sign(d)) % 4
        ref = w_at(t, plane, p, q, d * half, half if d == 0 else end)
        return send_to(ref, ref, gq2_s.at[t, i, d], gq2_r.at[t, i, d], along_last(t, sign(d)))

    def reduce_item(t, i):
        plane = (y + 1 + i // 4) % 2
        return plane, (first_of[t] + i + 1) % 4

    def span(d, far):
        if far:
            cut = (keep_r - 4 * GATHER_LATE) // 2
            return (0, cut) if d == 0 else (cut, keep_r - cut)
        return d * (kv // 2), kv // 2

    def rl(t, k):
        ref = part.at[t, k, :, pl.ds(keep_r, REDUCE_EARLY)]
        return send_to(ref, got_l.at[t, k], rl_s.at[t, k], rl_r.at[t, k], partner)

    def rq1(t, i, d, far):
        start, size = span(d, far)
        return send_to(
            part.at[t, i, (last_of[t] + 2) % 4, pl.ds(start, size)],
            got_a.at[t, i, d, pl.ds(0, size)],
            rq1_s.at[t, i, d], rq1_r.at[t, i, d], along_last(t, sign(d)),
        )

    def rq2(t, i, d, far):
        kept = pl.ds(0, keep_r if far else kv)
        return send_to(
            part.at[t, i, (last_of[t] + sign(d)) % 4, kept], got_b.at[t, i, d, kept],
            rq2_s.at[t, i, d], rq2_r.at[t, i, d], along_last(t, sign(d)),
        )

    def ry(t, k):
        kept = pl.ds(0, keep_r)
        return send_to(
            part.at[t, k, last_of[t], kept], got_y.at[t, k], ry_s.at[t, k], ry_r.at[t, k], partner
        )

    def rp1(t, d):
        start, size = span(d, False)
        return send_to(
            part.at[t, 5, last_of[t], pl.ds(start, size)], got_pa.at[t, d],
            rp1_s.at[t, d], rp1_r.at[t, d], along_first(t, sign(d)),
        )

    def rp2(t, d):
        return send_to(
            part.at[t, 4 if d == 0 else 6, last_of[t]], got_pb.at[t, d],
            rp2_s.at[t, d], rp2_r.at[t, d], along_first(t, sign(d)),
        )

    def by_plane(first_far, i, body):
        pl.when(i < N)(lambda: body(first_far))
        pl.when(i >= N)(lambda: body(not first_far))

    rep = lax.axis_index("replica")
    core = rep % 2
    other_core = rep + 1 - 2 * core
    other_chip = rep + 2 - 4 * (rep // 2)

    def frag_copy(k, src, dst, target):
        return pltpu.make_async_remote_copy(
            src_ref=src, dst_ref=dst, send_sem=frag_s.at[k], recv_sem=frag_r.at[k],
            device_id={"replica": target}, device_id_type=pl.DeviceIdType.MESH,
        )

    def frag_core():
        return frag_copy(0, pseudo, got_core, other_core)

    def frag_chip():
        return frag_copy(1, chip_sum, got_chip, other_chip)

    def frag_back():
        return frag_copy(2, frag_total.at[core], frag_total.at[core], other_core)

    types = (0, 1)
    ways = (0, 1)

    load_master = pltpu.make_async_copy(master_hbm, master, load_sem.at[0])
    load_cot = pltpu.make_async_copy(cot_hbm.at[0], cot, load_sem.at[1])
    plane_cols = act.shape[1] // 2

    def load_act(plane, slot):
        at = pl.ds(pl.multiple_of(plane * plane_cols, plane_cols), plane_cols)
        return pltpu.make_async_copy(act_hbm.at[0, :, at], act.at[:, at], load_sem.at[slot])

    load_frag = [
        pltpu.make_async_copy(outer_hbm, outer, load_sem.at[4]),
        pltpu.make_async_copy(local_hbm.at[0], local, load_sem.at[5]),
        pltpu.make_async_copy(moment_hbm, moment, load_sem.at[6]),
    ]
    load_adam = [
        pltpu.make_async_copy(first_hbm, first, load_sem.at[7]),
        pltpu.make_async_copy(second_hbm, second, load_sem.at[8]),
    ]
    load_master.start()
    load_cot.start()
    load_act(1 - y, 2).start()

    barrier = pltpu.get_barrier_semaphore()
    around = [along_first(0, 1), along_first(0, 3), along_last(0, 1), along_last(0, 3), partner]
    for other in around:
        pl.semaphore_signal(
            barrier, inc=1, device_id={"fsdp": other}, device_id_type=pl.DeviceIdType.MESH
        )
    for other in (other_core, other_chip):
        pl.semaphore_signal(
            barrier, inc=1, device_id={"replica": other}, device_id_type=pl.DeviceIdType.MESH
        )
    load_master.wait()
    for t in types:
        w[t, y, x, z] = master[0, :, t * kv:(t + 1) * kv].astype(BF16)
    pl.semaphore_wait(barrier, len(around) + 2)
    for t in types:
        for d in ways:
            gp1(t, d).start()
    for t in types:
        for d in ways:
            gq1(t, 0, d, False).start()
        gy(t, 0).start()
    load_act(y, 3).start()
    for load in load_frag + load_adam:
        load.start()

    load_cot.wait()
    for t in types:
        cot_t[pl.ds(t * kv, kv), :] = cot[:, t * kv:(t + 1) * kv].T
    for t in types:
        acc[t] = jnp.zeros(acc.shape[1:], F32)
    load_act(1 - y, 2).wait()

    def make_parts(i):
        for t in types:
            plane, p = reduce_item(t, i)
            if t == 0:
                at = pl.multiple_of((plane * 4 + p) * cols, cols)
                right = act[:, pl.ds(at, cols)]
            else:
                right = jnp.concatenate(
                    [
                        act[:, pl.ds(pl.multiple_of(device(plane, q, p) * rows, rows), rows)]
                        for q in range(N)
                    ],
                    axis=1,
                )
            for m in range(2):
                at = m * (kv // 2)
                prod = jnp.dot(
                    cot_t[pl.ds(t * kv + at, kv // 2), :], right, preferred_element_type=F32
                ).astype(BF16)
                for q in range(N):
                    part[t, i, q, pl.ds(at, kv // 2), :] = prod[:, q * rows:(q + 1) * rows]

    def add_half(t, i, d, far):
        start, size = span(d, far)
        at = pl.ds(start, size)
        q = (last_of[t] + sign(d)) % 4
        total = part[t, i, q, at, :].astype(F32) + got_a[t, i, d, pl.ds(0, size)].astype(F32)
        part[t, i, q, at, :] = total.astype(BF16)

    def project(i):
        for t in types:
            plane, p = gather_item(t, i)
            if t == 0:
                at = pl.multiple_of((plane * 4 + p) * cols, cols)
                left = act[:, pl.ds(at, cols)]
                right = w[t, plane, p]
            else:
                left = jnp.concatenate(
                    [
                        act[:, pl.ds(pl.multiple_of(device(plane, q, p) * rows, rows), rows)]
                        for q in range(N)
                    ],
                    axis=1,
                )
                right = w[t, plane, :, p]
            acc[t] += jnp.dot(left, right.reshape(cols, kv), preferred_element_type=F32)

    def input_grads(plane):
        def one(k, carry):
            b = plane * 4 + k
            at = pl.ds(pl.multiple_of(b * cols, cols), cols)
            total = None
            for t in types:
                term = lax.dot_general(
                    cot[:, t * kv:(t + 1) * kv], w[t, plane, k].reshape(cols, kv),
                    (((1,), (1,)), ((), ())),
                    preferred_element_type=F32,
                )
                total = term if total is None else total + term
            igrad[0, :, at] = total.astype(BF16)
            return carry

        lax.fori_loop(0, N, one, 0)

    def fragment_rounds(r):
        @pl.when(r == 1)
        def _():
            for load in load_frag:
                load.wait()
            pseudo[...] = (outer[1 - core] - local[1 - core]).astype(BF16)
            frag_core().start()

        @pl.when(r == 3)
        def _():
            frag_core().wait_recv()
            summed = outer[core] - local[core] + got_core[...].astype(F32)
            chip_sum[...] = summed.astype(BF16)
            frag_chip().start()

        @pl.when(r == 6)
        def _():
            frag_chip().wait_recv()
            frag_total[core] = chip_sum[...].astype(F32) + got_chip[...].astype(F32)
            frag_back().start()

        @pl.when(r == 7)
        def _():
            frag_back().wait_recv()
            for layer in range(2):
                mean = frag_total[layer] * (1.0 / N_REPLICA)
                new_moment = NESTEROV * moment[layer] + mean
                moment[layer] = new_moment
                outer[layer] = outer[layer] - OUTER_RATE * (mean + NESTEROV * new_moment)

    def round_of(r, carry):
        @pl.when(r == 1)
        def _():
            for t in types:
                for d in (1, 0):
                    gp1(t, d).wait_recv()
                    gp2(t, d).start()
                gy(t, 1).start()
                gy(t, 3).start()

        @pl.when(r == 2)
        def _():
            for t in types:
                for d in ways:
                    gp2(t, d).wait_recv()
                gy(t, 2).start()

        @pl.when((r >= 4) & (r < ITEMS))
        def _():
            for t in types:
                gy(t, r % 4).wait_recv()

        @pl.when((r >= 1) & (r < ITEMS))
        def _():
            @functools.partial(by_plane, False, r)
            def _(far):
                for t in types:
                    for d in ways:
                        gq1(t, r, d, far).start()

        @pl.when(r == LAG_G)
        def _():
            load_act(y, 3).wait()

        @pl.when(r < ITEMS)
        def _():
            make_parts(r)

            @functools.partial(by_plane, True, r)
            def _(far):
                for t in types:
                    if not far:
                        early = pl.ds(keep_r, REDUCE_EARLY)
                        rl(t, r % N).wait_recv()
                        both = part[t, r, :, early].astype(F32) + got_l[t, r % N].astype(F32)
                        part[t, r, :, early] = both.astype(BF16)
                    for d in ways:
                        rq1(t, r, d, far).start()
                    if far:
                        rl(t, r).start()

        fragment_rounds(r)

        @pl.when((r >= LAG_RQ2) & (r < ITEMS + LAG_RQ2))
        def _():
            i = r - LAG_RQ2

            @functools.partial(by_plane, True, i)
            def _(far):
                for t in types:
                    for d in ways:
                        rq1(t, i, d, far).wait_recv()
                        add_half(t, i, d, far)
                        rq2(t, i, d, far).start()

        @pl.when((r >= LAG_GQ2) & (r < ITEMS + LAG_GQ2))
        def _():
            i = r - LAG_GQ2

            @functools.partial(by_plane, False, i)
            def _(far):
                for t in types:
                    for d in ways:
                        gq1(t, i, d, far).wait_recv()
                        gq2(t, i, d, far).start()

        @pl.when((r >= LAG_RS) & (r < ITEMS + LAG_RS))
        def _():
            i = r - LAG_RS

            @functools.partial(by_plane, True, i)
            def _(far):
                for t in types:
                    q = last_of[t]
                    kept = pl.ds(0, keep_r if far else kv)
                    for d in ways:
                        rq2(t, i, d, far).wait_recv()
                    total = part[t, i, q, kept].astype(F32)
                    total += got_b[t, i, 0, kept].astype(F32)
                    total += got_b[t, i, 1, kept].astype(F32)
                    if far:
                        part[t, i, q, kept] = total.astype(BF16)
                        ry(t, i).start()
                    else:
                        ry(t, i % N).wait_recv()
                        mine[t] = total
                        mine[t, pl.ds(0, keep_r)] += got_y[t, i % N].astype(F32)

                        @pl.when(i < 7)
                        def _():
                            part[t, i, q] = mine[t].astype(BF16)

            @pl.when(i == 5)
            def _():
                for t in types:
                    for d in ways:
                        rp1(t, d).start()

            @pl.when(i == 6)
            def _():
                for t in types:
                    for d in ways:
                        rp1(t, d).wait_recv()
                        at = pl.ds(*span(d, False))
                        k = 4 if d == 0 else 6
                        total = part[t, k, last_of[t], at, :].astype(F32)
                        total += got_pa[t, d].astype(F32)
                        part[t, k, last_of[t], at, :] = total.astype(BF16)
                        rp2(t, d).start()

        @pl.when((r >= LAG_G) & (r < ITEMS + LAG_G))
        def _():
            i = r - LAG_G

            @functools.partial(by_plane, False, i)
            def _(far):
                for t in types:
                    for d in ways:
                        gq2(t, i, d, far).wait_recv()
                    if far:
                        gl(t, i % N).wait_recv()
                    else:
                        gl(t, i).start()

            project(i)

            @pl.when(i == 3)
            def _():
                input_grads(y)

            @pl.when(i == 7)
            def _():
                input_grads(1 - y)

        return carry

    lax.fori_loop(0, ROUNDS, round_of, 0)

    for t in types:
        out[0, :, t * kv:(t + 1) * kv] = acc[t].astype(BF16)
    for load in load_adam:
        load.wait()
    tokens = act.shape[0] * 32
    for t in types:
        for d in ways:
            rp2(t, d).wait_recv()
        total = mine[t] + got_pb[t, 0].astype(F32) + got_pb[t, 1].astype(F32)
        at = pl.ds(t * kv, kv)
        master[0, :, at], first[0, :, at], second[0, :, at] = adam_update(
            master[0, :, at], first[0, :, at], second[0, :, at],
            total.T * (1.0 / math.sqrt(tokens)),
        )

    for t in types:
        for d in ways:
            gp1(t, d).wait_send()
            gp2(t, d).wait_send()
            rp1(t, d).wait_send()
            rp2(t, d).wait_send()

    def drain(k, carry):
        for t in types:
            gy(t, k).wait_send()
            gl(t, k).wait_send()
            rl(t, k).wait_send()
            ry(t, k).wait_send()
            for d in ways:
                gq1(t, k, d, False).wait_send()
                gq2(t, k, d, False).wait_send()
                rq1(t, k, d, True).wait_send()
                rq2(t, k, d, True).wait_send()
                gq1(t, k + N, d, True).wait_send()
                gq2(t, k + N, d, True).wait_send()
                rq1(t, k + N, d, False).wait_send()
                rq2(t, k + N, d, False).wait_send()
        return carry

    for copy in (frag_core(), frag_chip(), frag_back()):
        copy.wait_send()
    lax.fori_loop(0, N, drain, 0)


def write_kernel(*refs):
    count = len(refs) // 2
    sem = refs[-1]
    copies = [
        pltpu.make_async_copy(refs[k], refs[count + k], sem.at[k]) for k in range(count)
    ]
    for copy in copies:
        copy.start()
    for copy in copies:
        copy.wait()


def write_out(results):
    return pl.pallas_call(
        write_kernel,
        out_shape=tuple(jax.ShapeDtypeStruct(r.shape, r.dtype) for r in results),
        in_specs=[pl.BlockSpec(memory_space=pltpu.VMEM)] * len(results),
        out_specs=tuple(pl.BlockSpec(memory_space=pl.ANY) for _ in results),
        scratch_shapes=[pltpu.SemaphoreType.DMA((len(results),))],
        compiler_params=pltpu.CompilerParams(vmem_limit_bytes=16 * 2**20),
        name="write_out",
    )(*results)


def train_step(activations, cotangent, master, outer, local, moment, first, second):
    tok, width = activations.shape[1:]
    kv2 = cotangent.shape[2]
    rows = master.shape[1]
    kv, kh = kv2 // 2, kv2 // 4
    dma = pltpu.SemaphoreType.DMA
    sems = []
    for shape in ((2, 2), (2, 2), (2, 4), (2, 8, 2), (2, 8, 2)):
        sems += [dma(shape), dma(shape)]
    for shape in ((2, 8, 2), (2, 8, 2), (2, 4), (2, 2), (2, 2)):
        sems += [dma(shape), dma(shape)]
    for shape in ((3,), (2, 4), (2, 4)):
        sems += [dma(shape), dma(shape)]
    layer = outer.shape[1:]
    hbm = pl.BlockSpec(memory_space=pl.ANY)
    return pl.pallas_call(
        train_kernel,
        out_shape=(
            pltpu.VMEM((1, tok, kv2), BF16),
            pltpu.VMEM((1, tok, width), BF16),
            pltpu.VMEM((1, rows, kv2), F32),
            pltpu.VMEM((1, rows, kv2), F32),
            pltpu.VMEM((1, rows, kv2), F32),
            pltpu.VMEM(outer.shape, F32),
            pltpu.VMEM(outer.shape, F32),
        ),
        in_specs=[hbm] * 8,
        out_specs=tuple(pl.BlockSpec(memory_space=pltpu.VMEM) for _ in range(7)),
        scratch_shapes=[
            pltpu.VMEM((tok, width), BF16),
            pltpu.VMEM((tok, kv2), BF16),
            pltpu.VMEM((kv2, tok), BF16),
            pltpu.VMEM((2, 2, N, N, rows, kv), BF16),
            pltpu.VMEM((2, 8, 4, kv, rows), BF16),
            pltpu.VMEM((2, 8, 2, kv - kv // 4, rows), BF16),
            pltpu.VMEM((2, 8, 2, kv, rows), BF16),
            pltpu.VMEM((2, 4, N, REDUCE_EARLY, rows), BF16),
            pltpu.VMEM((2, 4, kv - REDUCE_EARLY, rows), BF16),
            pltpu.VMEM((2, 2, kh, rows), BF16),
            pltpu.VMEM((2, 2, kv, rows), BF16),
            pltpu.VMEM((2, kv, rows), F32),
            pltpu.VMEM((2, tok, kv), F32),
            pltpu.VMEM((2, *layer), F32),
            pltpu.VMEM(layer, BF16),
            pltpu.VMEM(layer, BF16),
            pltpu.VMEM(layer, BF16),
            pltpu.VMEM(layer, BF16),
            pltpu.VMEM((2, *layer), F32),
            dma((9,)),
            *sems,
        ],
        compiler_params=pltpu.CompilerParams(
            collective_id=0, has_side_effects=True, vmem_limit_bytes=46 * 2**20
        ),
        cost_estimate=pl.CostEstimate(
            flops=6 * tok * width * kv2, bytes_accessed=100 * 2**20, transcendentals=0
        ),
        name="train_step",
    )(activations, cotangent, master, outer, local, moment, first, second)


def shards(
    activations,
    kv_cotangent,
    kv_master,
    kv_first,
    kv_second,
    outer_params,
    local_params,
    outer_momentum,
):
    return write_out(
        train_step(
            activations, kv_cotangent, kv_master, outer_params, local_params, outer_momentum,
            kv_first, kv_second,
        )
    )


def solution(mesh):
    row_split = P("replica", "fsdp", None)
    fragment = P(None, "fsdp", None)
    return jax.shard_map(
        shards,
        mesh=mesh,
        in_specs=(
            row_split,
            row_split,
            row_split,
            row_split,
            row_split,
            fragment,
            P("replica", None, "fsdp", None),
            fragment,
        ),
        out_specs=(row_split, row_split, row_split, row_split, row_split, fragment, fragment),
        check_vma=False,
    )
```

```python
import functools
import math

import jax
import jax.numpy as jnp
from jax import lax
from jax.experimental import pallas as pl
from jax.experimental.pallas import tpu as pltpu
from jax.sharding import PartitionSpec as P

FIRST_DECAY = 0.9
SECOND_DECAY = 0.95
ADAM_STEPS = 20.0
ADAM_EPSILON = 1e-08
INNER_RATE = 0.01
WEIGHT_DECAY = 0.1
NESTEROV = 0.9
OUTER_RATE = 0.7

BF16 = jnp.bfloat16
F32 = jnp.float32
N_REPLICA = 4
N = 4
ITEMS = 2 * N
SHIFT = 0
ROUNDS = ITEMS + 1 + SHIFT
GATHER_LATE = 16
REDUCE_EARLY = 64


def adam_update(master, first, second, grad):
    first = FIRST_DECAY * first + (1.0 - FIRST_DECAY) * grad
    second = SECOND_DECAY * second + (1.0 - SECOND_DECAY) * grad * grad
    first_fix = 1.0 - FIRST_DECAY**ADAM_STEPS
    second_fix = 1.0 - SECOND_DECAY**ADAM_STEPS
    update = first / first_fix / (jnp.sqrt(second / second_fix) + ADAM_EPSILON)
    master = master - INNER_RATE * (update + WEIGHT_DECAY * master)
    return (master, first, second)


def train_kernel(
    act_hbm,
    cot_hbm,
    master_hbm,
    outer_hbm,
    local_hbm,
    moment_hbm,
    first_hbm,
    second_hbm,
    out,
    igrad,
    master,
    first,
    second,
    outer,
    moment,
    act,
    cot,
    cot_t,
    w,
    part,
    got_a,
    got_b,
    got_l,
    got_y,
    got_pa,
    got_pb,
    mine,
    acc,
    local,
    pseudo,
    got_core,
    chip_sum,
    got_chip,
    frag_total,
    load_sem,
    gp1_s, gp1_r, gp2_s, gp2_r, gy_s, gy_r, gq1_s, gq1_r, gq2_s, gq2_r,
    rq1_s, rq1_r, rq2_s, rq2_r, ry_s, ry_r, rp1_s, rp1_r, rp2_s, rp2_r,
    frag_s, frag_r, gl_s, gl_r, rl_s, rl_r,
):
    f = lax.axis_index("fsdp")
    y, x, z = f // 16, (f // 4) % 4, f % 4
    first_of = (x, z)
    last_of = (z, x)
    rows, kv = w.shape[4:]
    half = rows // 2
    cols = N * rows
    keep_g = rows - GATHER_LATE
    keep_r = kv - REDUCE_EARLY

    def device(yy, xx, zz):
        return (yy * 4 + xx) * 4 + zz

    def along_first(t, step):
        p = (first_of[t] + step) % 4
        return device(y, p, z) if t == 0 else device(y, x, p)

    def along_last(t, step):
        q = (last_of[t] + step) % 4
        return device(y, x, q) if t == 0 else device(y, q, z)

    partner = device(1 - y, x, z)

    def send_to(src, dst, ss, rs, target):
        return pltpu.make_async_remote_copy(
            src_ref=src, dst_ref=dst, send_sem=ss, recv_sem=rs,
            device_id={"fsdp": target}, device_id_type=pl.DeviceIdType.MESH,
        )

    def w_at(t, plane, p, q, start=0, stop=rows):
        a, b = (p, q) if t == 0 else (q, p)
        return w.at[t, plane, a, b, pl.ds(start, stop - start)]

    def sign(d):
        return 1 if d == 0 else 3

    def gp1(t, d):
        own = w_at(t, y, first_of[t], last_of[t])
        return send_to(own, own, gp1_s.at[t, d], gp1_r.at[t, d], along_first(t, sign(d)))

    def gp2(t, d):
        ref = w_at(t, y, (first_of[t] + 4 - sign(d)) % 4, last_of[t], d * half, d * half + half)
        return send_to(ref, ref, gp2_s.at[t, d], gp2_r.at[t, d], along_first(t, sign(d)))

    def gy(t, k):
        ref = w_at(t, y, (first_of[t] + k) % 4, last_of[t], 0, keep_g)
        return send_to(ref, ref, gy_s.at[t, k], gy_r.at[t, k], partner)

    def gather_item(t, i):
        plane = (y + i // 4) % 2
        return plane, (first_of[t] + i) % 4

    def gl(t, k):
        p = (first_of[t] + k) % 4
        late = pl.ds(keep_g, GATHER_LATE)
        ref = w.at[0, y, p, :, late] if t == 0 else w.at[1, y, :, p, late]
        return send_to(ref, ref, gl_s.at[t, k], gl_r.at[t, k], partner)

    def gq1(t, i, d, far):
        plane, p = gather_item(t, i)
        ref = w_at(t, plane, p, last_of[t], 0, keep_g if far else rows)
        return send_to(ref, ref, gq1_s.at[t, i, d], gq1_r.at[t, i, d], along_last(t, sign(d)))

    def gq2(t, i, d, far):
        plane, p = gather_item(t, i)
        end = keep_g if far else rows
        q = (last_of[t] + 4 - sign(d)) % 4
        ref = w_at(t, plane, p, q, d * half, half if d == 0 else end)
        return send_to(ref, ref, gq2_s.at[t, i, d], gq2_r.at[t, i, d], along_last(t, sign(d)))

    def reduce_item(t, i):
        plane = (y + 1 + i // 4) % 2
        return plane, (first_of[t] + i + 1) % 4

    def span(d, far):
        if far:
            cut = (keep_r - 4 * GATHER_LATE) // 2
            return (0, cut) if d == 0 else (cut, keep_r - cut)
        return d * (kv // 2), kv // 2

    def rl(t, k):
        ref = part.at[t, k, :, pl.ds(keep_r, REDUCE_EARLY)]
        return send_to(ref, got_l.at[t, k], rl_s.at[t, k], rl_r.at[t, k], partner)

    def rq1(t, i, d, far):
        start, size = span(d, far)
        return send_to(
            part.at[t, i, (last_of[t] + 2) % 4, pl.ds(start, size)],
            got_a.at[t, i, d, pl.ds(0, size)],
            rq1_s.at[t, i, d], rq1_r.at[t, i, d], along_last(t, sign(d)),
        )

    def rq2(t, i, d, far):
        kept = pl.ds(0, keep_r if far else kv)
        return send_to(
            part.at[t, i, (last_of[t] + sign(d)) % 4, kept], got_b.at[t, i, d, kept],
            rq2_s.at[t, i, d], rq2_r.at[t, i, d], along_last(t, sign(d)),
        )

    def ry(t, k):
        kept = pl.ds(0, keep_r)
        return send_to(
            part.at[t, k, last_of[t], kept], got_y.at[t, k], ry_s.at[t, k], ry_r.at[t, k], partner
        )

    def rp1(t, d):
        start, size = span(d, False)
        return send_to(
            part.at[t, 5, last_of[t], pl.ds(start, size)], got_pa.at[t, d],
            rp1_s.at[t, d], rp1_r.at[t, d], along_first(t, sign(d)),
        )

    def rp2(t, d):
        return send_to(
            part.at[t, 4 if d == 0 else 6, last_of[t]], got_pb.at[t, d],
            rp2_s.at[t, d], rp2_r.at[t, d], along_first(t, sign(d)),
        )

    def by_plane(first_far, i, body):
        if isinstance(i, int):
            body(first_far if i < N else not first_far)
        else:
            pl.when(i < N)(lambda: body(first_far))
            pl.when(i >= N)(lambda: body(not first_far))

    rep = lax.axis_index("replica")
    core = rep % 2
    other_core = rep + 1 - 2 * core
    other_chip = rep + 2 - 4 * (rep // 2)

    def frag_copy(k, src, dst, target):
        return pltpu.make_async_remote_copy(
            src_ref=src, dst_ref=dst, send_sem=frag_s.at[k], recv_sem=frag_r.at[k],
            device_id={"replica": target}, device_id_type=pl.DeviceIdType.MESH,
        )

    def frag_core():
        return frag_copy(0, pseudo, got_core, other_core)

    def frag_chip():
        return frag_copy(1, chip_sum, got_chip, other_chip)

    def frag_back():
        return frag_copy(2, frag_total.at[core], frag_total.at[core], other_core)

    types = (0, 1)
    ways = (0, 1)

    load_master = pltpu.make_async_copy(master_hbm, master, load_sem.at[0])
    load_cot = pltpu.make_async_copy(cot_hbm.at[0], cot, load_sem.at[1])
    plane_cols = act.shape[1] // 2

    def load_act(plane, slot):
        at = pl.ds(pl.multiple_of(plane * plane_cols, plane_cols), plane_cols)
        return pltpu.make_async_copy(act_hbm.at[0, :, at], act.at[:, at], load_sem.at[slot])

    load_frag = [
        pltpu.make_async_copy(outer_hbm, outer, load_sem.at[4]),
        pltpu.make_async_copy(local_hbm.at[0], local, load_sem.at[5]),
        pltpu.make_async_copy(moment_hbm, moment, load_sem.at[6]),
    ]
    load_adam = [
        pltpu.make_async_copy(first_hbm, first, load_sem.at[7]),
        pltpu.make_async_copy(second_hbm, second, load_sem.at[8]),
    ]
    load_master.start()
    load_cot.start()
    load_act(1 - y, 2).start()

    barrier = pltpu.get_barrier_semaphore()
    around = [along_first(0, 1), along_first(0, 3), along_last(0, 1), along_last(0, 3), partner]
    for other in around:
        pl.semaphore_signal(
            barrier, inc=1, device_id={"fsdp": other}, device_id_type=pl.DeviceIdType.MESH
        )
    for other in (other_core, other_chip):
        pl.semaphore_signal(
            barrier, inc=1, device_id={"replica": other}, device_id_type=pl.DeviceIdType.MESH
        )
    load_master.wait()
    for t in types:
        w[t, y, x, z] = master[0, :, t * kv:(t + 1) * kv].astype(BF16)
    pl.semaphore_wait(barrier, len(around) + 2)
    for t in types:
        for d in ways:
            gp1(t, d).start()
    for t in types:
        for d in ways:
            gq1(t, 0, d, False).start()
        gy(t, 0).start()
    load_act(y, 3).start()
    for load in load_frag + load_adam:
        load.start()

    load_cot.wait()
    for t in types:
        cot_t[pl.ds(t * kv, kv), :] = cot[:, t * kv:(t + 1) * kv].T
    for t in types:
        acc[t] = jnp.zeros(acc.shape[1:], F32)
    load_act(1 - y, 2).wait()

    def make_parts(i):
        for t in types:
            plane, p = reduce_item(t, i)
            if t == 0:
                at = pl.multiple_of((plane * 4 + p) * cols, cols)
                right = act[:, pl.ds(at, cols)]
            else:
                right = jnp.concatenate(
                    [
                        act[:, pl.ds(pl.multiple_of(device(plane, q, p) * rows, rows), rows)]
                        for q in range(N)
                    ],
                    axis=1,
                )
            for m in range(2):
                at = m * (kv // 2)
                prod = jnp.dot(
                    cot_t[pl.ds(t * kv + at, kv // 2), :], right, preferred_element_type=F32
                ).astype(BF16)
                for q in range(N):
                    part[t, i, q, pl.ds(at, kv // 2), :] = prod[:, q * rows:(q + 1) * rows]

    def add_half(t, i, d, far):
        start, size = span(d, far)
        at = pl.ds(start, size)
        q = (last_of[t] + sign(d)) % 4
        total = part[t, i, q, at, :].astype(F32) + got_a[t, i, d, pl.ds(0, size)].astype(F32)
        part[t, i, q, at, :] = total.astype(BF16)

    def project(i, steps, last=False):
        for t in types:
            plane, p = gather_item(t, i)
            lefts, rights = [], []
            for step in steps:
                q = (last_of[t] + step) % 4
                b = device(plane, p, q) if t == 0 else device(plane, q, p)
                lefts.append(act[:, pl.ds(pl.multiple_of(b * rows, rows), rows)])
                rights.append(w_at(t, plane, p, q)[...])
            left = lefts[0] if len(lefts) == 1 else jnp.concatenate(lefts, axis=1)
            right = rights[0] if len(rights) == 1 else jnp.concatenate(rights, axis=0)
            term = jnp.dot(left, right, preferred_element_type=F32)
            if last:
                out[0, :, t * kv:(t + 1) * kv] = (acc[t] + term).astype(BF16)
            else:
                acc[t] += term

    def project_all(i):
        for t in types:
            plane, p = gather_item(t, i)
            if t == 0:
                at = pl.multiple_of((plane * 4 + p) * cols, cols)
                left = act[:, pl.ds(at, cols)]
                right = w[t, plane, p]
            else:
                left = jnp.concatenate(
                    [
                        act[:, pl.ds(pl.multiple_of(device(plane, q, p) * rows, rows), rows)]
                        for q in range(N)
                    ],
                    axis=1,
                )
                right = w[t, plane, :, p]
            acc[t] += jnp.dot(left, right.reshape(cols, kv), preferred_element_type=F32)

    def input_grad_blocks(plane, places):
        total = None
        for t in types:
            right = jnp.concatenate([w[t, plane, a, b] for a, b in places], axis=0)
            term = lax.dot_general(
                cot[:, t * kv:(t + 1) * kv], right, (((1,), (1,)), ((), ())),
                preferred_element_type=F32,
            )
            total = term if total is None else total + term
        total = total.astype(BF16)
        for k, (a, b) in enumerate(places):
            at = pl.ds(pl.multiple_of(device(plane, a, b) * rows, rows), rows)
            igrad[0, :, at] = total[:, k * rows:(k + 1) * rows]

    def input_grads(plane, start, count):
        def one(step, carry):
            k = (start + step) % 4
            b = plane * 4 + k
            at = pl.ds(pl.multiple_of(b * cols, cols), cols)
            total = None
            for t in types:
                term = lax.dot_general(
                    cot[:, t * kv:(t + 1) * kv], w[t, plane, k].reshape(cols, kv),
                    (((1,), (1,)), ((), ())),
                    preferred_element_type=F32,
                )
                total = term if total is None else total + term
            igrad[0, :, at] = total.astype(BF16)
            return carry

        lax.fori_loop(0, count, one, 0)

    def fragment_rounds(r):
        @pl.when(r == 1)
        def _():
            for load in load_frag:
                load.wait()
            pseudo[...] = (outer[1 - core] - local[1 - core]).astype(BF16)
            frag_core().start()

        @pl.when(r == 3)
        def _():
            frag_core().wait_recv()
            summed = outer[core] - local[core] + got_core[...].astype(F32)
            chip_sum[...] = summed.astype(BF16)
            frag_chip().start()

        @pl.when(r == 6)
        def _():
            frag_chip().wait_recv()
            frag_total[core] = chip_sum[...].astype(F32) + got_chip[...].astype(F32)
            frag_back().start()

        @pl.when(r == 7)
        def _():
            frag_back().wait_recv()
            for layer in range(2):
                mean = frag_total[layer] * (1.0 / N_REPLICA)
                new_moment = NESTEROV * moment[layer] + mean
                moment[layer] = new_moment
                outer[layer] = outer[layer] - OUTER_RATE * (mean + NESTEROV * new_moment)

    def finish_item(i):
        @functools.partial(by_plane, True, i)
        def _(far):
            for t in types:
                q = last_of[t]
                kept = pl.ds(0, keep_r if far else kv)
                for d in ways:
                    rq2(t, i, d, far).wait_recv()
                total = part[t, i, q, kept].astype(F32)
                total += got_b[t, i, 0, kept].astype(F32)
                total += got_b[t, i, 1, kept].astype(F32)
                if far:
                    part[t, i, q, kept] = total.astype(BF16)
                    ry(t, i).start()
                else:
                    ry(t, i % N).wait_recv()
                    mine[t] = total
                    mine[t, pl.ds(0, keep_r)] += got_y[t, i % N].astype(F32)

                    def keep():
                        part[t, i, q] = mine[t].astype(BF16)

                    if not isinstance(i, int):
                        pl.when(i < 7)(keep)

        if isinstance(i, int):
            return

        @pl.when(i == 5)
        def _():
            for t in types:
                for d in ways:
                    rp1(t, d).start()

        @pl.when(i == 6)
        def _():
            for t in types:
                for d in ways:
                    rp1(t, d).wait_recv()
                    at = pl.ds(*span(d, False))
                    k = 4 if d == 0 else 6
                    total = part[t, k, last_of[t], at, :].astype(F32)
                    total += got_pa[t, d].astype(F32)
                    part[t, k, last_of[t], at, :] = total.astype(BF16)
                    rp2(t, d).start()

    def round_of(r, carry):
        @pl.when(r == 2)
        def _():
            load_act(y, 3).wait()

        @pl.when(r < ITEMS)
        def _():
            make_parts(r)

            @functools.partial(by_plane, True, r)
            def _(far):
                for t in types:
                    if not far:
                        early = pl.ds(keep_r, REDUCE_EARLY)
                        rl(t, r % N).wait_recv()
                        both = part[t, r, :, early].astype(F32) + got_l[t, r % N].astype(F32)
                        part[t, r, :, early] = both.astype(BF16)
                    for d in ways:
                        rq1(t, r, d, far).start()
                    if far:
                        rl(t, r).start()

        @pl.when(r == 1)
        def _():
            for t in types:
                for d in (1, 0):
                    gp1(t, d).wait_recv()
                    gp2(t, d).start()
                gy(t, 1).start()
                gy(t, 3).start()

        @pl.when(r == 2)
        def _():
            for t in types:
                for d in ways:
                    gp2(t, d).wait_recv()
                gy(t, 2).start()

        g = r - SHIFT

        @pl.when((g >= 1) & (g < ITEMS))
        def _():
            @functools.partial(by_plane, False, g)
            def _(far):
                for t in types:
                    if far:
                        gy(t, g % N).wait_recv()
                    for d in ways:
                        gq1(t, g, d, far).start()

        fragment_rounds(r)

        @pl.when((r >= 1) & (r < ITEMS + 1))
        def _():
            i = r - 1

            @functools.partial(by_plane, True, i)
            def _(far):
                for t in types:
                    for d in ways:
                        rq1(t, i, d, far).wait_recv()
                        add_half(t, i, d, far)
                        rq2(t, i, d, far).start()

        @pl.when((g >= 1) & (g < ITEMS + 1))
        def _():
            i = g - 1

            @functools.partial(by_plane, False, i)
            def _(far):
                for t in types:
                    for d in ways:
                        gq1(t, i, d, far).wait_recv()
                        gq2(t, i, d, far).start()

        @pl.when((r >= 2) & (r < ITEMS + 2))
        def _():
            finish_item(r - 2)

        @pl.when(g >= 2)
        def _():
            i = g - 2

            @functools.partial(by_plane, False, i)
            def _(far):
                for t in types:
                    for d in ways:
                        gq2(t, i, d, far).wait_recv()
                    if far:
                        gl(t, i % N).wait_recv()
                    else:
                        gl(t, i).start()

            project_all(i)

            @pl.when(i == 3)
            def _():
                input_grads(y, 0, N)

        return carry

    lax.fori_loop(0, ROUNDS, round_of, 0)

    def reduce_end():
        if SHIFT == 0:
            finish_item(7)
        for load in load_adam:
            load.wait()
        tokens = act.shape[0] * 32
        for t in types:
            for d in ways:
                rp2(t, d).wait_recv()
            total = mine[t] + got_pb[t, 0].astype(F32) + got_pb[t, 1].astype(F32)
            at = pl.ds(t * kv, kv)
            master[0, :, at], first[0, :, at], second[0, :, at] = adam_update(
                master[0, :, at], first[0, :, at], second[0, :, at],
                total.T * (1.0 / math.sqrt(tokens)),
            )

    if SHIFT:
        reduce_end()
    for t in types:
        gl(t, 3).wait_recv()
    far_plane = 1 - y
    xs, zs = [(x + k) % 4 for k in range(N)], [(z + k) % 4 for k in range(N)]
    project(7, (0, 1, 3))
    input_grads(far_plane, x, 2)
    input_grad_blocks(far_plane, [(xs[2], zs[k]) for k in (0, 1, 2)])
    input_grad_blocks(far_plane, [(xs[3], zs[k]) for k in (0, 1, 3)])
    if not SHIFT:
        reduce_end()
    for t in types:
        for d in ways:
            gq2(t, 7, d, True).wait_recv()
    project(7, (2,), True)
    input_grad_blocks(far_plane, [(xs[3], zs[2]), (xs[2], zs[3])])
    for t in types:
        for d in ways:
            gp1(t, d).wait_send()
            gp2(t, d).wait_send()
            rp1(t, d).wait_send()
            rp2(t, d).wait_send()

    def drain(k, carry):
        for t in types:
            gy(t, k).wait_send()
            gl(t, k).wait_send()
            rl(t, k).wait_send()
            ry(t, k).wait_send()
            for d in ways:
                gq1(t, k, d, False).wait_send()
                gq2(t, k, d, False).wait_send()
                rq1(t, k, d, True).wait_send()
                rq2(t, k, d, True).wait_send()
                gq1(t, k + N, d, True).wait_send()
                gq2(t, k + N, d, True).wait_send()
                rq1(t, k + N, d, False).wait_send()
                rq2(t, k + N, d, False).wait_send()
        return carry

    for copy in (frag_core(), frag_chip(), frag_back()):
        copy.wait_send()
    lax.fori_loop(0, N, drain, 0)


def write_kernel(*refs):
    count = len(refs) // 2
    sem = refs[-1]
    copies = []
    for k in range(count):
        lines = refs[k].shape[1]
        pieces = 4 if k == 1 else 2
        for piece in range(pieces):
            at = pl.ds(piece * (lines // pieces), lines // pieces)
            copies.append(
                pltpu.make_async_copy(
                    refs[k].at[:, at], refs[count + k].at[:, at], sem.at[len(copies)]
                )
            )
    for copy in copies:
        copy.start()
    for copy in copies:
        copy.wait()


def write_out(results):
    return pl.pallas_call(
        write_kernel,
        out_shape=tuple(jax.ShapeDtypeStruct(r.shape, r.dtype) for r in results),
        in_specs=[pl.BlockSpec(memory_space=pltpu.VMEM)] * len(results),
        out_specs=tuple(pl.BlockSpec(memory_space=pl.ANY) for _ in results),
        scratch_shapes=[pltpu.SemaphoreType.DMA((2 * len(results) + 2,))],
        compiler_params=pltpu.CompilerParams(vmem_limit_bytes=16 * 2**20),
        name="write_out",
    )(*results)


def train_step(activations, cotangent, master, outer, local, moment, first, second):
    tok, width = activations.shape[1:]
    kv2 = cotangent.shape[2]
    rows = master.shape[1]
    kv, kh = kv2 // 2, kv2 // 4
    dma = pltpu.SemaphoreType.DMA
    sems = []
    for shape in ((2, 2), (2, 2), (2, 4), (2, 8, 2), (2, 8, 2)):
        sems += [dma(shape), dma(shape)]
    for shape in ((2, 8, 2), (2, 8, 2), (2, 4), (2, 2), (2, 2)):
        sems += [dma(shape), dma(shape)]
    for shape in ((3,), (2, 4), (2, 4)):
        sems += [dma(shape), dma(shape)]
    layer = outer.shape[1:]
    hbm = pl.BlockSpec(memory_space=pl.ANY)
    return pl.pallas_call(
        train_kernel,
        out_shape=(
            pltpu.VMEM((1, tok, kv2), BF16),
            pltpu.VMEM((1, tok, width), BF16),
            pltpu.VMEM((1, rows, kv2), F32),
            pltpu.VMEM((1, rows, kv2), F32),
            pltpu.VMEM((1, rows, kv2), F32),
            pltpu.VMEM(outer.shape, F32),
            pltpu.VMEM(outer.shape, F32),
        ),
        in_specs=[hbm] * 8,
        out_specs=tuple(pl.BlockSpec(memory_space=pltpu.VMEM) for _ in range(7)),
        scratch_shapes=[
            pltpu.VMEM((tok, width), BF16),
            pltpu.VMEM((tok, kv2), BF16),
            pltpu.VMEM((kv2, tok), BF16),
            pltpu.VMEM((2, 2, N, N, rows, kv), BF16),
            pltpu.VMEM((2, 8, 4, kv, rows), BF16),
            pltpu.VMEM((2, 8, 2, kv - kv // 4, rows), BF16),
            pltpu.VMEM((2, 8, 2, kv, rows), BF16),
            pltpu.VMEM((2, 4, N, REDUCE_EARLY, rows), BF16),
            pltpu.VMEM((2, 4, kv - REDUCE_EARLY, rows), BF16),
            pltpu.VMEM((2, 2, kh, rows), BF16),
            pltpu.VMEM((2, 2, kv, rows), BF16),
            pltpu.VMEM((2, kv, rows), F32),
            pltpu.VMEM((2, tok, kv), F32),
            pltpu.VMEM((2, *layer), F32),
            pltpu.VMEM(layer, BF16),
            pltpu.VMEM(layer, BF16),
            pltpu.VMEM(layer, BF16),
            pltpu.VMEM(layer, BF16),
            pltpu.VMEM((2, *layer), F32),
            dma((9,)),
            *sems,
        ],
        compiler_params=pltpu.CompilerParams(
            collective_id=0, has_side_effects=True, vmem_limit_bytes=46 * 2**20
        ),
        cost_estimate=pl.CostEstimate(
            flops=6 * tok * width * kv2, bytes_accessed=100 * 2**20, transcendentals=0
        ),
        name="train_step",
    )(activations, cotangent, master, outer, local, moment, first, second)


def shards(
    activations,
    kv_cotangent,
    kv_master,
    kv_first,
    kv_second,
    outer_params,
    local_params,
    outer_momentum,
):
    return write_out(
        train_step(
            activations, kv_cotangent, kv_master, outer_params, local_params, outer_momentum,
            kv_first, kv_second,
        )
    )


def solution(mesh):
    row_split = P("replica", "fsdp", None)
    fragment = P(None, "fsdp", None)
    return jax.shard_map(
        shards,
        mesh=mesh,
        in_specs=(
            row_split,
            row_split,
            row_split,
            row_split,
            row_split,
            fragment,
            P("replica", None, "fsdp", None),
            fragment,
        ),
        out_specs=(row_split, row_split, row_split, row_split, row_split, fragment, fragment),
        check_vma=False,
    )
```

```python
import functools
import math

import jax
import jax.numpy as jnp
from jax import lax
from jax.experimental import pallas as pl
from jax.experimental.pallas import tpu as pltpu
from jax.sharding import PartitionSpec as P

FIRST_DECAY = 0.9
SECOND_DECAY = 0.95
ADAM_STEPS = 20.0
ADAM_EPSILON = 1e-08
INNER_RATE = 0.01
WEIGHT_DECAY = 0.1
NESTEROV = 0.9
OUTER_RATE = 0.7

BF16 = jnp.bfloat16
F32 = jnp.float32
N_REPLICA = 4
N = 4
ITEMS = 2 * N
SHIFT = 0
ROUNDS = ITEMS + 1 + SHIFT
GATHER_LATE = 16
REDUCE_EARLY = 64


def adam_update(master, first, second, grad):
    first = FIRST_DECAY * first + (1.0 - FIRST_DECAY) * grad
    second = SECOND_DECAY * second + (1.0 - SECOND_DECAY) * grad * grad
    first_fix = 1.0 - FIRST_DECAY**ADAM_STEPS
    second_fix = 1.0 - SECOND_DECAY**ADAM_STEPS
    update = first / first_fix / (jnp.sqrt(second / second_fix) + ADAM_EPSILON)
    master = master - INNER_RATE * (update + WEIGHT_DECAY * master)
    return (master, first, second)


def train_kernel(
    act_hbm,
    cot_hbm,
    master_hbm,
    outer_hbm,
    local_hbm,
    moment_hbm,
    first_hbm,
    second_hbm,
    igrad,
    master,
    first,
    second,
    outer,
    moment,
    act,
    cot,
    w,
    acc,
    mine,
    got_pb,
    cot_t,
    part,
    got_a,
    got_b,
    got_l,
    got_y,
    got_pa,
    local,
    pseudo,
    got_core,
    chip_sum,
    got_chip,
    frag_total,
    load_sem,
    gp1_s, gp1_r, gp2_s, gp2_r, gy_s, gy_r, gq1_s, gq1_r, gq2_s, gq2_r,
    rq1_s, rq1_r, rq2_s, rq2_r, ry_s, ry_r, rp1_s, rp1_r, rp2_s, rp2_r,
    frag_s, frag_r, gl_s, gl_r, rl_s, rl_r,
):
    f = lax.axis_index("fsdp")
    y, x, z = f // 16, (f // 4) % 4, f % 4
    first_of = (x, z)
    last_of = (z, x)
    rows, kv = w.shape[4:]
    half = rows // 2
    cols = N * rows
    keep_g = rows - GATHER_LATE
    keep_r = kv - REDUCE_EARLY

    def device(yy, xx, zz):
        return (yy * 4 + xx) * 4 + zz

    def along_first(t, step):
        p = (first_of[t] + step) % 4
        return device(y, p, z) if t == 0 else device(y, x, p)

    def along_last(t, step):
        q = (last_of[t] + step) % 4
        return device(y, x, q) if t == 0 else device(y, q, z)

    partner = device(1 - y, x, z)

    def send_to(src, dst, ss, rs, target):
        return pltpu.make_async_remote_copy(
            src_ref=src, dst_ref=dst, send_sem=ss, recv_sem=rs,
            device_id={"fsdp": target}, device_id_type=pl.DeviceIdType.MESH,
        )

    def w_at(t, plane, p, q, start=0, stop=rows):
        a, b = (p, q) if t == 0 else (q, p)
        return w.at[t, plane, a, b, pl.ds(start, stop - start)]

    def sign(d):
        return 1 if d == 0 else 3

    def gp1(t, d):
        own = w_at(t, y, first_of[t], last_of[t])
        return send_to(own, own, gp1_s.at[t, d], gp1_r.at[t, d], along_first(t, sign(d)))

    def gp2(t, d):
        ref = w_at(t, y, (first_of[t] + 4 - sign(d)) % 4, last_of[t], d * half, d * half + half)
        return send_to(ref, ref, gp2_s.at[t, d], gp2_r.at[t, d], along_first(t, sign(d)))

    def gy(t, k):
        ref = w_at(t, y, (first_of[t] + k) % 4, last_of[t], 0, keep_g)
        return send_to(ref, ref, gy_s.at[t, k], gy_r.at[t, k], partner)

    def gather_item(t, i):
        plane = (y + i // 4) % 2
        return plane, (first_of[t] + i) % 4

    def gl(t, k):
        p = (first_of[t] + k) % 4
        late = pl.ds(keep_g, GATHER_LATE)
        ref = w.at[0, y, p, :, late] if t == 0 else w.at[1, y, :, p, late]
        return send_to(ref, ref, gl_s.at[t, k], gl_r.at[t, k], partner)

    def gq1(t, i, d, far):
        plane, p = gather_item(t, i)
        ref = w_at(t, plane, p, last_of[t], 0, keep_g if far else rows)
        return send_to(ref, ref, gq1_s.at[t, i, d], gq1_r.at[t, i, d], along_last(t, sign(d)))

    def gq2(t, i, d, far):
        plane, p = gather_item(t, i)
        end = keep_g if far else rows
        q = (last_of[t] + 4 - sign(d)) % 4
        ref = w_at(t, plane, p, q, d * half, half if d == 0 else end)
        return send_to(ref, ref, gq2_s.at[t, i, d], gq2_r.at[t, i, d], along_last(t, sign(d)))

    def reduce_item(t, i):
        plane = (y + 1 + i // 4) % 2
        return plane, (first_of[t] + i + 1) % 4

    def span(d, far):
        if far:
            cut = (keep_r - 4 * GATHER_LATE) // 2
            return (0, cut) if d == 0 else (cut, keep_r - cut)
        return d * (kv // 2), kv // 2

    def rl(t, k):
        ref = part.at[t, k, :, pl.ds(keep_r, REDUCE_EARLY)]
        return send_to(ref, got_l.at[t, k], rl_s.at[t, k], rl_r.at[t, k], partner)

    def rq1(t, i, d, far):
        start, size = span(d, far)
        return send_to(
            part.at[t, i, (last_of[t] + 2) % 4, pl.ds(start, size)],
            got_a.at[t, i, d, pl.ds(0, size)],
            rq1_s.at[t, i, d], rq1_r.at[t, i, d], along_last(t, sign(d)),
        )

    def rq2(t, i, d, far):
        kept = pl.ds(0, keep_r if far else kv)
        return send_to(
            part.at[t, i, (last_of[t] + sign(d)) % 4, kept], got_b.at[t, i, d, kept],
            rq2_s.at[t, i, d], rq2_r.at[t, i, d], along_last(t, sign(d)),
        )

    def ry(t, k):
        kept = pl.ds(0, keep_r)
        return send_to(
            part.at[t, k, last_of[t], kept], got_y.at[t, k], ry_s.at[t, k], ry_r.at[t, k], partner
        )

    def rp1(t, d):
        start, size = span(d, False)
        return send_to(
            part.at[t, 5, last_of[t], pl.ds(start, size)], got_pa.at[t, d],
            rp1_s.at[t, d], rp1_r.at[t, d], along_first(t, sign(d)),
        )

    def rp2(t, d):
        return send_to(
            part.at[t, 4 if d == 0 else 6, last_of[t]], got_pb.at[t, d],
            rp2_s.at[t, d], rp2_r.at[t, d], along_first(t, sign(d)),
        )

    def by_plane(first_far, i, body):
        if isinstance(i, int):
            body(first_far if i < N else not first_far)
        else:
            pl.when(i < N)(lambda: body(first_far))
            pl.when(i >= N)(lambda: body(not first_far))

    rep = lax.axis_index("replica")
    core = rep % 2
    other_core = rep + 1 - 2 * core
    other_chip = rep + 2 - 4 * (rep // 2)

    def frag_copy(k, src, dst, target):
        return pltpu.make_async_remote_copy(
            src_ref=src, dst_ref=dst, send_sem=frag_s.at[k], recv_sem=frag_r.at[k],
            device_id={"replica": target}, device_id_type=pl.DeviceIdType.MESH,
        )

    def frag_core():
        return frag_copy(0, pseudo, got_core, other_core)

    def frag_chip():
        return frag_copy(1, chip_sum, got_chip, other_chip)

    def frag_back():
        return frag_copy(2, frag_total.at[core], frag_total.at[core], other_core)

    types = (0, 1)
    ways = (0, 1)

    load_master = pltpu.make_async_copy(master_hbm, master, load_sem.at[0])
    load_cot = pltpu.make_async_copy(cot_hbm.at[0], cot, load_sem.at[1])
    plane_cols = act.shape[1] // 2

    def load_act(plane, slot):
        at = pl.ds(pl.multiple_of(plane * plane_cols, plane_cols), plane_cols)
        return pltpu.make_async_copy(act_hbm.at[0, :, at], act.at[:, at], load_sem.at[slot])

    load_frag = [
        pltpu.make_async_copy(outer_hbm, outer, load_sem.at[4]),
        pltpu.make_async_copy(local_hbm.at[0], local, load_sem.at[5]),
        pltpu.make_async_copy(moment_hbm, moment, load_sem.at[6]),
    ]
    load_adam = [
        pltpu.make_async_copy(first_hbm, first, load_sem.at[7]),
        pltpu.make_async_copy(second_hbm, second, load_sem.at[8]),
    ]
    load_master.start()
    load_cot.start()
    load_act(1 - y, 2).start()

    barrier = pltpu.get_barrier_semaphore()
    around = [along_first(0, 1), along_first(0, 3), along_last(0, 1), along_last(0, 3), partner]
    for other in around:
        pl.semaphore_signal(
            barrier, inc=1, device_id={"fsdp": other}, device_id_type=pl.DeviceIdType.MESH
        )
    for other in (other_core, other_chip):
        pl.semaphore_signal(
            barrier, inc=1, device_id={"replica": other}, device_id_type=pl.DeviceIdType.MESH
        )
    load_master.wait()
    for t in types:
        w[t, y, x, z] = master[0, :, t * kv:(t + 1) * kv].astype(BF16)
    pl.semaphore_wait(barrier, len(around) + 2)
    for t in types:
        for d in ways:
            gp1(t, d).start()
    for t in types:
        for d in ways:
            gq1(t, 0, d, False).start()
        gy(t, 0).start()
    load_act(y, 3).start()
    for load in load_frag + load_adam:
        load.start()

    load_cot.wait()
    for t in types:
        cot_t[pl.ds(t * kv, kv), :] = cot[:, t * kv:(t + 1) * kv].T
    for t in types:
        acc[t] = jnp.zeros(acc.shape[1:], F32)
    load_act(1 - y, 2).wait()

    def make_parts(i):
        for t in types:
            plane, p = reduce_item(t, i)
            if t == 0:
                at = pl.multiple_of((plane * 4 + p) * cols, cols)
                right = act[:, pl.ds(at, cols)]
            else:
                right = jnp.concatenate(
                    [
                        act[:, pl.ds(pl.multiple_of(device(plane, q, p) * rows, rows), rows)]
                        for q in range(N)
                    ],
                    axis=1,
                )
            for m in range(2):
                at = m * (kv // 2)
                prod = jnp.dot(
                    cot_t[pl.ds(t * kv + at, kv // 2), :], right, preferred_element_type=F32
                ).astype(BF16)
                for q in range(N):
                    part[t, i, q, pl.ds(at, kv // 2), :] = prod[:, q * rows:(q + 1) * rows]

    def add_half(t, i, d, far):
        start, size = span(d, far)
        at = pl.ds(start, size)
        q = (last_of[t] + sign(d)) % 4
        total = part[t, i, q, at, :].astype(F32) + got_a[t, i, d, pl.ds(0, size)].astype(F32)
        part[t, i, q, at, :] = total.astype(BF16)

    def project(i, steps):
        for t in types:
            plane, p = gather_item(t, i)
            lefts, rights = [], []
            for step in steps:
                q = (last_of[t] + step) % 4
                b = device(plane, p, q) if t == 0 else device(plane, q, p)
                lefts.append(act[:, pl.ds(pl.multiple_of(b * rows, rows), rows)])
                rights.append(w_at(t, plane, p, q)[...])
            left = lefts[0] if len(lefts) == 1 else jnp.concatenate(lefts, axis=1)
            right = rights[0] if len(rights) == 1 else jnp.concatenate(rights, axis=0)
            acc[t] += jnp.dot(left, right, preferred_element_type=F32)

    def project_all(i):
        for t in types:
            plane, p = gather_item(t, i)
            if t == 0:
                at = pl.multiple_of((plane * 4 + p) * cols, cols)
                left = act[:, pl.ds(at, cols)]
                right = w[t, plane, p]
            else:
                left = jnp.concatenate(
                    [
                        act[:, pl.ds(pl.multiple_of(device(plane, q, p) * rows, rows), rows)]
                        for q in range(N)
                    ],
                    axis=1,
                )
                right = w[t, plane, :, p]
            acc[t] += jnp.dot(left, right.reshape(cols, kv), preferred_element_type=F32)

    def input_grad_blocks(plane, places):
        total = None
        for t in types:
            right = jnp.concatenate([w[t, plane, a, b] for a, b in places], axis=0)
            term = lax.dot_general(
                cot[:, t * kv:(t + 1) * kv], right, (((1,), (1,)), ((), ())),
                preferred_element_type=F32,
            )
            total = term if total is None else total + term
        total = total.astype(BF16)
        for k, (a, b) in enumerate(places):
            at = pl.ds(pl.multiple_of(device(plane, a, b) * rows, rows), rows)
            igrad[0, :, at] = total[:, k * rows:(k + 1) * rows]

    def input_grads(plane, start, count):
        def one(step, carry):
            k = (start + step) % 4
            b = plane * 4 + k
            at = pl.ds(pl.multiple_of(b * cols, cols), cols)
            total = None
            for t in types:
                term = lax.dot_general(
                    cot[:, t * kv:(t + 1) * kv], w[t, plane, k].reshape(cols, kv),
                    (((1,), (1,)), ((), ())),
                    preferred_element_type=F32,
                )
                total = term if total is None else total + term
            igrad[0, :, at] = total.astype(BF16)
            return carry

        lax.fori_loop(0, count, one, 0)

    def fragment_rounds(r):
        @pl.when(r == 1)
        def _():
            for load in load_frag:
                load.wait()
            pseudo[...] = (outer[1 - core] - local[1 - core]).astype(BF16)
            frag_core().start()

        @pl.when(r == 3)
        def _():
            frag_core().wait_recv()
            summed = outer[core] - local[core] + got_core[...].astype(F32)
            chip_sum[...] = summed.astype(BF16)
            frag_chip().start()

        @pl.when(r == 6)
        def _():
            frag_chip().wait_recv()
            frag_total[core] = chip_sum[...].astype(F32) + got_chip[...].astype(F32)
            frag_back().start()

        @pl.when(r == 7)
        def _():
            frag_back().wait_recv()
            for layer in range(2):
                mean = frag_total[layer] * (1.0 / N_REPLICA)
                new_moment = NESTEROV * moment[layer] + mean
                moment[layer] = new_moment
                outer[layer] = outer[layer] - OUTER_RATE * (mean + NESTEROV * new_moment)

    def finish_item(i):
        @functools.partial(by_plane, True, i)
        def _(far):
            for t in types:
                q = last_of[t]
                kept = pl.ds(0, keep_r if far else kv)
                for d in ways:
                    rq2(t, i, d, far).wait_recv()
                total = part[t, i, q, kept].astype(F32)
                total += got_b[t, i, 0, kept].astype(F32)
                total += got_b[t, i, 1, kept].astype(F32)
                if far:
                    part[t, i, q, kept] = total.astype(BF16)
                    ry(t, i).start()
                else:
                    ry(t, i % N).wait_recv()
                    mine[t] = total
                    mine[t, pl.ds(0, keep_r)] += got_y[t, i % N].astype(F32)

                    def keep():
                        part[t, i, q] = mine[t].astype(BF16)

                    if not isinstance(i, int):
                        pl.when(i < 7)(keep)

        if isinstance(i, int):
            return

        @pl.when(i == 5)
        def _():
            for t in types:
                for d in ways:
                    rp1(t, d).start()

        @pl.when(i == 6)
        def _():
            for t in types:
                for d in ways:
                    rp1(t, d).wait_recv()
                    at = pl.ds(*span(d, False))
                    k = 4 if d == 0 else 6
                    total = part[t, k, last_of[t], at, :].astype(F32)
                    total += got_pa[t, d].astype(F32)
                    part[t, k, last_of[t], at, :] = total.astype(BF16)
                    rp2(t, d).start()

    def round_of(r, carry):
        @pl.when(r == 2)
        def _():
            load_act(y, 3).wait()

        @pl.when(r < ITEMS)
        def _():
            make_parts(r)

            @functools.partial(by_plane, True, r)
            def _(far):
                for t in types:
                    if not far:
                        early = pl.ds(keep_r, REDUCE_EARLY)
                        rl(t, r % N).wait_recv()
                        both = part[t, r, :, early].astype(F32) + got_l[t, r % N].astype(F32)
                        part[t, r, :, early] = both.astype(BF16)
                    for d in ways:
                        rq1(t, r, d, far).start()
                    if far:
                        rl(t, r).start()

        @pl.when(r == 1)
        def _():
            for t in types:
                for d in (1, 0):
                    gp1(t, d).wait_recv()
                    gp2(t, d).start()
                gy(t, 1).start()
                gy(t, 3).start()

        @pl.when(r == 2)
        def _():
            for t in types:
                for d in ways:
                    gp2(t, d).wait_recv()
                gy(t, 2).start()

        g = r - SHIFT

        @pl.when((g >= 1) & (g < ITEMS))
        def _():
            @functools.partial(by_plane, False, g)
            def _(far):
                for t in types:
                    if far:
                        gy(t, g % N).wait_recv()
                    for d in ways:
                        gq1(t, g, d, far).start()

        fragment_rounds(r)

        @pl.when((r >= 1) & (r < ITEMS + 1))
        def _():
            i = r - 1

            @functools.partial(by_plane, True, i)
            def _(far):
                for t in types:
                    for d in ways:
                        rq1(t, i, d, far).wait_recv()
                        add_half(t, i, d, far)
                        rq2(t, i, d, far).start()

        @pl.when((g >= 1) & (g < ITEMS + 1))
        def _():
            i = g - 1

            @functools.partial(by_plane, False, i)
            def _(far):
                for t in types:
                    for d in ways:
                        gq1(t, i, d, far).wait_recv()
                        gq2(t, i, d, far).start()

        @pl.when((r >= 2) & (r < ITEMS + 2))
        def _():
            finish_item(r - 2)

        @pl.when(g >= 2)
        def _():
            i = g - 2

            @functools.partial(by_plane, False, i)
            def _(far):
                for t in types:
                    for d in ways:
                        gq2(t, i, d, far).wait_recv()
                    if far:
                        gl(t, i % N).wait_recv()
                    else:
                        gl(t, i).start()

            project_all(i)

            @pl.when(i == 3)
            def _():
                input_grads(y, 0, N)

        return carry

    lax.fori_loop(0, ROUNDS, round_of, 0)

    for t in types:
        gl(t, 3).wait_recv()
    far_plane = 1 - y
    xs, zs = [(x + k) % 4 for k in range(N)], [(z + k) % 4 for k in range(N)]
    project(7, (0, 1, 3))
    input_grads(far_plane, x, 2)
    input_grad_blocks(far_plane, [(xs[2], zs[k]) for k in (0, 1, 2)])
    input_grad_blocks(far_plane, [(xs[3], zs[k]) for k in (0, 1, 3)])
    for load in load_adam:
        load.wait()
    finish_item(7)
    for t in types:
        for d in ways:
            rp2(t, d).wait_recv()
            gq2(t, 7, d, True).wait_recv()

    for t in types:
        for d in ways:
            gp1(t, d).wait_send()
            gp2(t, d).wait_send()
            rp1(t, d).wait_send()
            rp2(t, d).wait_send()

    def drain(k, carry):
        for t in types:
            gy(t, k).wait_send()
            gl(t, k).wait_send()
            rl(t, k).wait_send()
            ry(t, k).wait_send()
            for d in ways:
                gq1(t, k, d, False).wait_send()
                gq2(t, k, d, False).wait_send()
                rq1(t, k, d, True).wait_send()
                rq2(t, k, d, True).wait_send()
                gq1(t, k + N, d, True).wait_send()
                gq2(t, k + N, d, True).wait_send()
                rq1(t, k + N, d, False).wait_send()
                rq2(t, k + N, d, False).wait_send()
        return carry

    for copy in (frag_core(), frag_chip(), frag_back()):
        copy.wait_send()
    lax.fori_loop(0, N, drain, 0)


def finish_kernel(
    igrad, master, first, second, outer, moment, act, cot, w, acc, mine, got_pb,
    out_hbm, igrad_hbm, master_hbm, first_hbm, second_hbm, outer_hbm, moment_hbm,
    out, last, new_master, new_first, new_second, sem,
):
    f = lax.axis_index("fsdp")
    y, x, z = f // 16, (f // 4) % 4, f % 4
    rows, kv = w.shape[4:]
    cols = N * rows
    plane = 1 - y
    started = []

    def put(src, dst):
        copy = pltpu.make_async_copy(src, dst, sem.at[len(started)])
        copy.start()
        started.append(copy)

    def columns(start, size):
        return pl.ds(pl.multiple_of(start, size), size)

    def block(a, b):
        return columns(((plane * 4 + a) * 4 + b) * rows, rows)

    def put_igrad(at):
        put(igrad.at[0, :, at], igrad_hbm.at[0, :, at])

    xs, zs = [(x + k) % 4 for k in range(N)], [(z + k) % 4 for k in range(N)]
    put(outer, outer_hbm)
    put(moment, moment_hbm)
    put_igrad(columns(y * N * cols, N * cols))
    for k in (0, 1):
        put_igrad(columns((plane * 4 + xs[k]) * cols, cols))
    for k in (0, 1, 2):
        put_igrad(block(xs[2], zs[k]))
    for k in (0, 1, 3):
        put_igrad(block(xs[3], zs[k]))

    places = ((xs[3], zs[2]), (xs[2], zs[3]))
    for t, (a, b) in enumerate(places):
        at = slice(t * kv, (t + 1) * kv)
        total = acc[t] + jnp.dot(act[:, block(a, b)], w[t, plane, a, b], preferred_element_type=F32)
        out[:, at] = total.astype(BF16)
        put(out.at[:, at], out_hbm.at[0, :, at])
    total = None
    for t in (0, 1):
        right = jnp.concatenate([w[t, plane, a, b] for a, b in places], axis=0)
        term = lax.dot_general(
            cot[:, t * kv:(t + 1) * kv], right, (((1,), (1,)), ((), ())),
            preferred_element_type=F32,
        )
        total = term if total is None else total + term
    last[...] = total.astype(BF16)
    for k, (a, b) in enumerate(places):
        put(last.at[:, k * rows:(k + 1) * rows], igrad_hbm.at[0, :, block(a, b)])

    tokens = act.shape[0] * 32
    for t in (0, 1):
        total = mine[t] + got_pb[t, 0].astype(F32) + got_pb[t, 1].astype(F32)
        at = slice(t * kv, (t + 1) * kv)
        new_master[:, at], new_first[:, at], new_second[:, at] = adam_update(
            master[0, :, at], first[0, :, at], second[0, :, at],
            total.T * (1.0 / math.sqrt(tokens)),
        )
        for src, dst in (
            (new_master, master_hbm), (new_first, first_hbm), (new_second, second_hbm)
        ):
            put(src.at[:, at], dst.at[0, :, at])
    for copy in started:
        copy.wait()


def finish(tok, kv2, rows, *held):
    igrad, master, first, second, outer, moment = held[:6]
    hbm = pl.BlockSpec(memory_space=pl.ANY)
    results = [jax.ShapeDtypeStruct((1, tok, kv2), BF16)]
    results += [
        jax.ShapeDtypeStruct(r.shape, r.dtype)
        for r in (igrad, master, first, second, outer, moment)
    ]
    return pl.pallas_call(
        finish_kernel,
        out_shape=tuple(results),
        in_specs=[pl.BlockSpec(memory_space=pltpu.VMEM)] * len(held),
        out_specs=(hbm,) * len(results),
        scratch_shapes=[
            pltpu.VMEM((tok, kv2), BF16),
            pltpu.VMEM((tok, 2 * rows), BF16),
            pltpu.VMEM((rows, kv2), F32),
            pltpu.VMEM((rows, kv2), F32),
            pltpu.VMEM((rows, kv2), F32),
            pltpu.SemaphoreType.DMA((21,)),
        ],
        compiler_params=pltpu.CompilerParams(vmem_limit_bytes=16 * 2**20),
        name="finish",
    )(*held)


def train_step(activations, cotangent, master, outer, local, moment, first, second):
    tok, width = activations.shape[1:]
    kv2 = cotangent.shape[2]
    rows = master.shape[1]
    kv, kh = kv2 // 2, kv2 // 4
    dma = pltpu.SemaphoreType.DMA
    sems = []
    for shape in ((2, 2), (2, 2), (2, 4), (2, 8, 2), (2, 8, 2)):
        sems += [dma(shape), dma(shape)]
    for shape in ((2, 8, 2), (2, 8, 2), (2, 4), (2, 2), (2, 2)):
        sems += [dma(shape), dma(shape)]
    for shape in ((3,), (2, 4), (2, 4)):
        sems += [dma(shape), dma(shape)]
    layer = outer.shape[1:]
    hbm = pl.BlockSpec(memory_space=pl.ANY)
    return pl.pallas_call(
        train_kernel,
        out_shape=(
            pltpu.VMEM((1, tok, width), BF16),
            pltpu.VMEM((1, rows, kv2), F32),
            pltpu.VMEM((1, rows, kv2), F32),
            pltpu.VMEM((1, rows, kv2), F32),
            pltpu.VMEM(outer.shape, F32),
            pltpu.VMEM(outer.shape, F32),
            pltpu.VMEM((tok, width), BF16),
            pltpu.VMEM((tok, kv2), BF16),
            pltpu.VMEM((2, 2, N, N, rows, kv), BF16),
            pltpu.VMEM((2, tok, kv), F32),
            pltpu.VMEM((2, kv, rows), F32),
            pltpu.VMEM((2, 2, kv, rows), BF16),
        ),
        in_specs=[hbm] * 8,
        out_specs=tuple(pl.BlockSpec(memory_space=pltpu.VMEM) for _ in range(12)),
        scratch_shapes=[
            pltpu.VMEM((kv2, tok), BF16),
            pltpu.VMEM((2, 8, 4, kv, rows), BF16),
            pltpu.VMEM((2, 8, 2, kv - kv // 4, rows), BF16),
            pltpu.VMEM((2, 8, 2, kv, rows), BF16),
            pltpu.VMEM((2, 4, N, REDUCE_EARLY, rows), BF16),
            pltpu.VMEM((2, 4, kv - REDUCE_EARLY, rows), BF16),
            pltpu.VMEM((2, 2, kh, rows), BF16),
            pltpu.VMEM((2, *layer), F32),
            pltpu.VMEM(layer, BF16),
            pltpu.VMEM(layer, BF16),
            pltpu.VMEM(layer, BF16),
            pltpu.VMEM(layer, BF16),
            pltpu.VMEM((2, *layer), F32),
            dma((9,)),
            *sems,
        ],
        compiler_params=pltpu.CompilerParams(
            collective_id=0, has_side_effects=True, vmem_limit_bytes=30 * 2**20
        ),
        cost_estimate=pl.CostEstimate(
            flops=6 * tok * width * kv2, bytes_accessed=100 * 2**20, transcendentals=0
        ),
        name="train_step",
    )(activations, cotangent, master, outer, local, moment, first, second)


def shards(
    activations,
    kv_cotangent,
    kv_master,
    kv_first,
    kv_second,
    outer_params,
    local_params,
    outer_momentum,
):
    held = train_step(
        activations, kv_cotangent, kv_master, outer_params, local_params, outer_momentum,
        kv_first, kv_second,
    )
    return finish(activations.shape[1], kv_cotangent.shape[2], kv_master.shape[1], *held)


def solution(mesh):
    row_split = P("replica", "fsdp", None)
    fragment = P(None, "fsdp", None)
    return jax.shard_map(
        shards,
        mesh=mesh,
        in_specs=(
            row_split,
            row_split,
            row_split,
            row_split,
            row_split,
            fragment,
            P("replica", None, "fsdp", None),
            fragment,
        ),
        out_specs=(row_split, row_split, row_split, row_split, row_split, fragment, fragment),
        check_vma=False,
    )
```

```python
import functools
import math

import jax
import jax.numpy as jnp
from jax import lax
from jax.experimental import pallas as pl
from jax.experimental.pallas import tpu as pltpu
from jax.sharding import PartitionSpec as P

FIRST_DECAY = 0.9
SECOND_DECAY = 0.95
ADAM_STEPS = 20.0
ADAM_EPSILON = 1e-08
INNER_RATE = 0.01
WEIGHT_DECAY = 0.1
NESTEROV = 0.9
OUTER_RATE = 0.7

BF16 = jnp.bfloat16
F32 = jnp.float32
N_REPLICA = 4
N = 4
ITEMS = 2 * N
SHIFT = 0
ROUNDS = ITEMS + 1 + SHIFT
PIECE_ROWS = 64
GATHER_LATE = 16
REDUCE_EARLY = 64


def adam_update(master, first, second, grad):
    first = FIRST_DECAY * first + (1.0 - FIRST_DECAY) * grad
    second = SECOND_DECAY * second + (1.0 - SECOND_DECAY) * grad * grad
    first_fix = 1.0 - FIRST_DECAY**ADAM_STEPS
    second_fix = 1.0 - SECOND_DECAY**ADAM_STEPS
    update = first / first_fix / (jnp.sqrt(second / second_fix) + ADAM_EPSILON)
    master = master - INNER_RATE * (update + WEIGHT_DECAY * master)
    return (master, first, second)


class Pieces:
    def __init__(self, remote, shape):
        self.remote, self.shape = remote, shape

    def wait_recv(self):
        self.remote(None).wait_recv()

    def wait_send(self):
        self.remote(None).wait_send()

    def start(self):
        count = self.shape[0]
        step = 1 if len(self.shape) == 3 else PIECE_ROWS
        for at in range(0, count, step):
            self.remote(pl.ds(at, min(step, count - at))).start()


def train_kernel(
    act_hbm,
    cot_hbm,
    master_hbm,
    outer_hbm,
    local_hbm,
    moment_hbm,
    first_hbm,
    second_hbm,
    igrad,
    master,
    first,
    second,
    outer,
    moment,
    act,
    cot,
    w,
    acc,
    mine,
    got_pb,
    cot_t,
    part,
    got_a,
    got_b,
    got_l,
    got_y,
    got_pa,
    local,
    pseudo,
    got_core,
    chip_sum,
    got_chip,
    frag_total,
    load_sem,
    gp1_s, gp1_r, gp2_s, gp2_r, gy_s, gy_r, gq1_s, gq1_r, gq2_s, gq2_r,
    rq1_s, rq1_r, rq2_s, rq2_r, ry_s, ry_r, rp1_s, rp1_r, rp2_s, rp2_r,
    frag_s, frag_r, gl_s, gl_r, rl_s, rl_r,
):
    f = lax.axis_index("fsdp")
    y, x, z = f // 16, (f // 4) % 4, f % 4
    first_of = (x, z)
    last_of = (z, x)
    rows, kv = w.shape[4:]
    half = rows // 2
    cols = N * rows
    keep_g = rows - GATHER_LATE
    keep_r = kv - REDUCE_EARLY

    def device(yy, xx, zz):
        return (yy * 4 + xx) * 4 + zz

    def along_first(t, step):
        p = (first_of[t] + step) % 4
        return device(y, p, z) if t == 0 else device(y, x, p)

    def along_last(t, step):
        q = (last_of[t] + step) % 4
        return device(y, x, q) if t == 0 else device(y, q, z)

    partner = device(1 - y, x, z)

    def send_to(src, dst, ss, rs, target):
        def remote(at):
            return pltpu.make_async_remote_copy(
                src_ref=src if at is None else src.at[at], dst_ref=dst if at is None else dst.at[at],
                send_sem=ss, recv_sem=rs,
                device_id={"fsdp": target}, device_id_type=pl.DeviceIdType.MESH,
            )

        return Pieces(remote, src.shape)

    def w_at(t, plane, p, q, start=0, stop=rows):
        a, b = (p, q) if t == 0 else (q, p)
        return w.at[t, plane, a, b, pl.ds(start, stop - start)]

    def sign(d):
        return 1 if d == 0 else 3

    def gp1(t, d):
        own = w_at(t, y, first_of[t], last_of[t])
        return send_to(own, own, gp1_s.at[t, d], gp1_r.at[t, d], along_first(t, sign(d)))

    def gp2(t, d):
        ref = w_at(t, y, (first_of[t] + 4 - sign(d)) % 4, last_of[t], d * half, d * half + half)
        return send_to(ref, ref, gp2_s.at[t, d], gp2_r.at[t, d], along_first(t, sign(d)))

    def gy(t, k):
        ref = w_at(t, y, (first_of[t] + k) % 4, last_of[t], 0, keep_g)
        return send_to(ref, ref, gy_s.at[t, k], gy_r.at[t, k], partner)

    def gather_item(t, i):
        plane = (y + i // 4) % 2
        return plane, (first_of[t] + i) % 4

    def gl(t, k):
        p = (first_of[t] + k) % 4
        late = pl.ds(keep_g, GATHER_LATE)
        ref = w.at[0, y, p, :, late] if t == 0 else w.at[1, y, :, p, late]
        return send_to(ref, ref, gl_s.at[t, k], gl_r.at[t, k], partner)

    def gq1(t, i, d, far):
        plane, p = gather_item(t, i)
        ref = w_at(t, plane, p, last_of[t], 0, keep_g if far else rows)
        return send_to(ref, ref, gq1_s.at[t, i, d], gq1_r.at[t, i, d], along_last(t, sign(d)))

    def gq2(t, i, d, far):
        plane, p = gather_item(t, i)
        end = keep_g if far else rows
        q = (last_of[t] + 4 - sign(d)) % 4
        ref = w_at(t, plane, p, q, d * half, half if d == 0 else end)
        return send_to(ref, ref, gq2_s.at[t, i, d], gq2_r.at[t, i, d], along_last(t, sign(d)))

    def reduce_item(t, i):
        plane = (y + 1 + i // 4) % 2
        return plane, (first_of[t] + i + 1) % 4

    def span(d, far):
        if far:
            cut = (keep_r - 4 * GATHER_LATE) // 2
            return (0, cut) if d == 0 else (cut, keep_r - cut)
        return d * (kv // 2), kv // 2

    def rl(t, k):
        ref = part.at[t, k, :, pl.ds(keep_r, REDUCE_EARLY)]
        return send_to(ref, got_l.at[t, k], rl_s.at[t, k], rl_r.at[t, k], partner)

    def rq1(t, i, d, far):
        start, size = span(d, far)
        return send_to(
            part.at[t, i, (last_of[t] + 2) % 4, pl.ds(start, size)],
            got_a.at[t, i, d, pl.ds(0, size)],
            rq1_s.at[t, i, d], rq1_r.at[t, i, d], along_last(t, sign(d)),
        )

    def rq2(t, i, d, far):
        kept = pl.ds(0, keep_r if far else kv)
        return send_to(
            part.at[t, i, (last_of[t] + sign(d)) % 4, kept], got_b.at[t, i, d, kept],
            rq2_s.at[t, i, d], rq2_r.at[t, i, d], along_last(t, sign(d)),
        )

    def ry(t, k):
        kept = pl.ds(0, keep_r)
        return send_to(
            part.at[t, k, last_of[t], kept], got_y.at[t, k], ry_s.at[t, k], ry_r.at[t, k], partner
        )

    def rp1(t, d):
        start, size = span(d, False)
        return send_to(
            part.at[t, 5, last_of[t], pl.ds(start, size)], got_pa.at[t, d],
            rp1_s.at[t, d], rp1_r.at[t, d], along_first(t, sign(d)),
        )

    def rp2(t, d):
        return send_to(
            part.at[t, 4 if d == 0 else 6, last_of[t]], got_pb.at[t, d],
            rp2_s.at[t, d], rp2_r.at[t, d], along_first(t, sign(d)),
        )

    def by_plane(first_far, i, body):
        if isinstance(i, int):
            body(first_far if i < N else not first_far)
        else:
            pl.when(i < N)(lambda: body(first_far))
            pl.when(i >= N)(lambda: body(not first_far))

    rep = lax.axis_index("replica")
    core = rep % 2
    other_core = rep + 1 - 2 * core
    other_chip = rep + 2 - 4 * (rep // 2)

    def frag_copy(k, src, dst, target):
        return pltpu.make_async_remote_copy(
            src_ref=src, dst_ref=dst, send_sem=frag_s.at[k], recv_sem=frag_r.at[k],
            device_id={"replica": target}, device_id_type=pl.DeviceIdType.MESH,
        )

    def frag_core():
        return frag_copy(0, pseudo, got_core, other_core)

    def frag_chip():
        return frag_copy(1, chip_sum, got_chip, other_chip)

    def frag_back():
        return frag_copy(2, frag_total.at[core], frag_total.at[core], other_core)

    types = (0, 1)
    ways = (0, 1)

    def load_master(t):
        at = pl.ds(t * kv, kv)
        return pltpu.make_async_copy(
            master_hbm.at[:, :, at], master.at[:, :, at], load_sem.at[(0, 9)[t]]
        )

    load_cot = pltpu.make_async_copy(cot_hbm.at[0], cot, load_sem.at[1])
    plane_cols = act.shape[1] // 2

    def load_act(plane, slot):
        at = pl.ds(pl.multiple_of(plane * plane_cols, plane_cols), plane_cols)
        return pltpu.make_async_copy(act_hbm.at[0, :, at], act.at[:, at], load_sem.at[slot])

    load_frag = [
        pltpu.make_async_copy(outer_hbm, outer, load_sem.at[4]),
        pltpu.make_async_copy(local_hbm.at[0], local, load_sem.at[5]),
        pltpu.make_async_copy(moment_hbm, moment, load_sem.at[6]),
    ]
    load_adam = [
        pltpu.make_async_copy(first_hbm, first, load_sem.at[7]),
        pltpu.make_async_copy(second_hbm, second, load_sem.at[8]),
    ]
    for t in types:
        load_master(t).start()
    load_cot.start()
    load_act(1 - y, 2).start()

    barrier = pltpu.get_barrier_semaphore()
    around = [along_first(0, 1), along_first(0, 3), along_last(0, 1), along_last(0, 3), partner]
    for other in around:
        pl.semaphore_signal(
            barrier, inc=1, device_id={"fsdp": other}, device_id_type=pl.DeviceIdType.MESH
        )
    for other in (other_core, other_chip):
        pl.semaphore_signal(
            barrier, inc=1, device_id={"replica": other}, device_id_type=pl.DeviceIdType.MESH
        )
    for t in types:
        load_master(t).wait()
        w[t, y, x, z] = master[0, :, t * kv:(t + 1) * kv].astype(BF16)
        if t == 0:
            pl.semaphore_wait(barrier, len(around) + 2)
        for d in ways:
            gp1(t, d).start()
            gq1(t, 0, d, False).start()
        gy(t, 0).start()
    load_act(y, 3).start()
    for load in load_frag + load_adam:
        load.start()

    load_cot.wait()
    for t in types:
        cot_t[pl.ds(t * kv, kv), :] = cot[:, t * kv:(t + 1) * kv].T
    for t in types:
        acc[t] = jnp.zeros(acc.shape[1:], F32)
    load_act(1 - y, 2).wait()

    def make_parts(i):
        for t in types:
            plane, p = reduce_item(t, i)
            if t == 0:
                at = pl.multiple_of((plane * 4 + p) * cols, cols)
                right = act[:, pl.ds(at, cols)]
            else:
                right = jnp.concatenate(
                    [
                        act[:, pl.ds(pl.multiple_of(device(plane, q, p) * rows, rows), rows)]
                        for q in range(N)
                    ],
                    axis=1,
                )
            for m in range(2):
                at = m * (kv // 2)
                prod = jnp.dot(
                    cot_t[pl.ds(t * kv + at, kv // 2), :], right, preferred_element_type=F32
                ).astype(BF16)
                for q in range(N):
                    part[t, i, q, pl.ds(at, kv // 2), :] = prod[:, q * rows:(q + 1) * rows]

    def add_half(t, i, d, far):
        start, size = span(d, far)
        at = pl.ds(start, size)
        q = (last_of[t] + sign(d)) % 4
        total = part[t, i, q, at, :].astype(F32) + got_a[t, i, d, pl.ds(0, size)].astype(F32)
        part[t, i, q, at, :] = total.astype(BF16)

    def project(i, steps):
        for t in types:
            plane, p = gather_item(t, i)
            lefts, rights = [], []
            for step in steps:
                q = (last_of[t] + step) % 4
                b = device(plane, p, q) if t == 0 else device(plane, q, p)
                lefts.append(act[:, pl.ds(pl.multiple_of(b * rows, rows), rows)])
                rights.append(w_at(t, plane, p, q)[...])
            left = lefts[0] if len(lefts) == 1 else jnp.concatenate(lefts, axis=1)
            right = rights[0] if len(rights) == 1 else jnp.concatenate(rights, axis=0)
            acc[t] += jnp.dot(left, right, preferred_element_type=F32)

    def project_all(i):
        for t in types:
            plane, p = gather_item(t, i)
            if t == 0:
                at = pl.multiple_of((plane * 4 + p) * cols, cols)
                left = act[:, pl.ds(at, cols)]
                right = w[t, plane, p]
            else:
                left = jnp.concatenate(
                    [
                        act[:, pl.ds(pl.multiple_of(device(plane, q, p) * rows, rows), rows)]
                        for q in range(N)
                    ],
                    axis=1,
                )
                right = w[t, plane, :, p]
            acc[t] += jnp.dot(left, right.reshape(cols, kv), preferred_element_type=F32)

    def input_grad_blocks(plane, places):
        total = None
        for t in types:
            right = jnp.concatenate([w[t, plane, a, b] for a, b in places], axis=0)
            term = lax.dot_general(
                cot[:, t * kv:(t + 1) * kv], right, (((1,), (1,)), ((), ())),
                preferred_element_type=F32,
            )
            total = term if total is None else total + term
        total = total.astype(BF16)
        for k, (a, b) in enumerate(places):
            at = pl.ds(pl.multiple_of(device(plane, a, b) * rows, rows), rows)
            igrad[0, :, at] = total[:, k * rows:(k + 1) * rows]

    def input_grads(plane, start, count):
        def one(step, carry):
            k = (start + step) % 4
            b = plane * 4 + k
            at = pl.ds(pl.multiple_of(b * cols, cols), cols)
            total = None
            for t in types:
                term = lax.dot_general(
                    cot[:, t * kv:(t + 1) * kv], w[t, plane, k].reshape(cols, kv),
                    (((1,), (1,)), ((), ())),
                    preferred_element_type=F32,
                )
                total = term if total is None else total + term
            igrad[0, :, at] = total.astype(BF16)
            return carry

        lax.fori_loop(0, count, one, 0)

    def fragment_rounds(r):
        @pl.when(r == 1)
        def _():
            for load in load_frag:
                load.wait()
            pseudo[...] = (outer[1 - core] - local[1 - core]).astype(BF16)
            frag_core().start()

        @pl.when(r == 2)
        def _():
            frag_core().wait_recv()
            summed = outer[core] - local[core] + got_core[...].astype(F32)
            chip_sum[...] = summed.astype(BF16)
            frag_chip().start()

        @pl.when(r == 6)
        def _():
            frag_chip().wait_recv()
            frag_total[core] = chip_sum[...].astype(F32) + got_chip[...].astype(F32)
            frag_back().start()

        @pl.when(r == 7)
        def _():
            frag_back().wait_recv()
            for layer in range(2):
                mean = frag_total[layer] * (1.0 / N_REPLICA)
                new_moment = NESTEROV * moment[layer] + mean
                moment[layer] = new_moment
                outer[layer] = outer[layer] - OUTER_RATE * (mean + NESTEROV * new_moment)

    def finish_item(i):
        @functools.partial(by_plane, True, i)
        def _(far):
            for t in types:
                q = last_of[t]
                kept = pl.ds(0, keep_r if far else kv)
                for d in ways:
                    rq2(t, i, d, far).wait_recv()
                total = part[t, i, q, kept].astype(F32)
                total += got_b[t, i, 0, kept].astype(F32)
                total += got_b[t, i, 1, kept].astype(F32)
                if far:
                    part[t, i, q, kept] = total.astype(BF16)
                    ry(t, i).start()
                else:
                    ry(t, i % N).wait_recv()
                    mine[t] = total
                    mine[t, pl.ds(0, keep_r)] += got_y[t, i % N].astype(F32)

                    def keep():
                        part[t, i, q] = mine[t].astype(BF16)

                    if not isinstance(i, int):
                        pl.when(i < 7)(keep)

        if isinstance(i, int):
            return

        @pl.when(i == 5)
        def _():
            for t in types:
                for d in ways:
                    rp1(t, d).start()

        @pl.when(i == 6)
        def _():
            for t in types:
                for d in ways:
                    rp1(t, d).wait_recv()
                    at = pl.ds(*span(d, False))
                    k = 4 if d == 0 else 6
                    total = part[t, k, last_of[t], at, :].astype(F32)
                    total += got_pa[t, d].astype(F32)
                    part[t, k, last_of[t], at, :] = total.astype(BF16)
                    rp2(t, d).start()

    def round_of(r, carry):
        @pl.when(r == 2)
        def _():
            load_act(y, 3).wait()

        @pl.when(r < ITEMS)
        def _():
            make_parts(r)

            @functools.partial(by_plane, True, r)
            def _(far):
                for t in types:
                    if not far:
                        early = pl.ds(keep_r, REDUCE_EARLY)
                        rl(t, r % N).wait_recv()
                        both = part[t, r, :, early].astype(F32) + got_l[t, r % N].astype(F32)
                        part[t, r, :, early] = both.astype(BF16)
                    for d in ways:
                        rq1(t, r, d, far).start()
                    if far:
                        rl(t, r).start()

        @pl.when(r == 1)
        def _():
            for t in types:
                for d in (1, 0):
                    gp1(t, d).wait_recv()
                    gp2(t, d).start()
                gy(t, 1).start()
                gy(t, 3).start()

        @pl.when(r == 2)
        def _():
            for t in types:
                for d in ways:
                    gp2(t, d).wait_recv()
                gy(t, 2).start()

        g = r - SHIFT

        @pl.when((g >= 1) & (g < ITEMS))
        def _():
            @functools.partial(by_plane, False, g)
            def _(far):
                for t in types:
                    if far:
                        gy(t, g % N).wait_recv()
                    for d in ways:
                        gq1(t, g, d, far).start()

        fragment_rounds(r)

        @pl.when((r >= 1) & (r < ITEMS + 1))
        def _():
            i = r - 1

            @functools.partial(by_plane, True, i)
            def _(far):
                for t in types:
                    for d in ways:
                        rq1(t, i, d, far).wait_recv()
                        add_half(t, i, d, far)
                        rq2(t, i, d, far).start()

        @pl.when((g >= 1) & (g < ITEMS + 1))
        def _():
            i = g - 1

            @functools.partial(by_plane, False, i)
            def _(far):
                for t in types:
                    for d in ways:
                        gq1(t, i, d, far).wait_recv()
                        gq2(t, i, d, far).start()

        @pl.when((r >= 2) & (r < ITEMS + 2))
        def _():
            finish_item(r - 2)

        @pl.when(g >= 2)
        def _():
            i = g - 2

            @functools.partial(by_plane, False, i)
            def _(far):
                for t in types:
                    for d in ways:
                        gq2(t, i, d, far).wait_recv()
                    if far:
                        gl(t, i % N).wait_recv()
                    else:
                        gl(t, i).start()

            project_all(i)

            @pl.when(i == 3)
            def _():
                input_grads(y, 0, N)

        return carry

    lax.fori_loop(0, ROUNDS, round_of, 0)

    for t in types:
        gl(t, 3).wait_recv()
    far_plane = 1 - y
    xs, zs = [(x + k) % 4 for k in range(N)], [(z + k) % 4 for k in range(N)]
    project(7, (0, 1, 3))
    input_grads(far_plane, x, 2)
    input_grad_blocks(far_plane, [(xs[2], zs[k]) for k in (0, 1, 2)])
    input_grad_blocks(far_plane, [(xs[3], zs[k]) for k in (0, 1, 3)])
    for load in load_adam:
        load.wait()
    finish_item(7)
    for t in types:
        for d in ways:
            rp2(t, d).wait_recv()
            gq2(t, 7, d, True).wait_recv()

    for t in types:
        for d in ways:
            gp1(t, d).wait_send()
            gp2(t, d).wait_send()
            rp1(t, d).wait_send()
            rp2(t, d).wait_send()

    def drain(k, carry):
        for t in types:
            gy(t, k).wait_send()
            gl(t, k).wait_send()
            rl(t, k).wait_send()
            ry(t, k).wait_send()
            for d in ways:
                gq1(t, k, d, False).wait_send()
                gq2(t, k, d, False).wait_send()
                rq1(t, k, d, True).wait_send()
                rq2(t, k, d, True).wait_send()
                gq1(t, k + N, d, True).wait_send()
                gq2(t, k + N, d, True).wait_send()
                rq1(t, k + N, d, False).wait_send()
                rq2(t, k + N, d, False).wait_send()
        return carry

    for copy in (frag_core(), frag_chip(), frag_back()):
        copy.wait_send()
    lax.fori_loop(0, N, drain, 0)


def finish_kernel(
    igrad, master, first, second, outer, moment, act, cot, w, acc, mine, got_pb,
    out_hbm, igrad_hbm, master_hbm, first_hbm, second_hbm, outer_hbm, moment_hbm,
    out, last, new_master, new_first, new_second, sem,
):
    f = lax.axis_index("fsdp")
    y, x, z = f // 16, (f // 4) % 4, f % 4
    rows, kv = w.shape[4:]
    cols = N * rows
    plane = 1 - y
    started = []

    def put(src, dst):
        copy = pltpu.make_async_copy(src, dst, sem.at[len(started)])
        copy.start()
        started.append(copy)

    def columns(start, size):
        return pl.ds(pl.multiple_of(start, size), size)

    def block(a, b):
        return columns(((plane * 4 + a) * 4 + b) * rows, rows)

    def put_igrad(at):
        put(igrad.at[0, :, at], igrad_hbm.at[0, :, at])

    xs, zs = [(x + k) % 4 for k in range(N)], [(z + k) % 4 for k in range(N)]
    put(outer, outer_hbm)
    put(moment, moment_hbm)
    put_igrad(columns(y * N * cols, N * cols))
    for k in (0, 1):
        put_igrad(columns((plane * 4 + xs[k]) * cols, cols))
    for k in (0, 1, 2):
        put_igrad(block(xs[2], zs[k]))
    for k in (0, 1, 3):
        put_igrad(block(xs[3], zs[k]))

    places = ((xs[3], zs[2]), (xs[2], zs[3]))
    for t, (a, b) in enumerate(places):
        at = slice(t * kv, (t + 1) * kv)
        total = acc[t] + jnp.dot(act[:, block(a, b)], w[t, plane, a, b], preferred_element_type=F32)
        out[:, at] = total.astype(BF16)
        put(out.at[:, at], out_hbm.at[0, :, at])
    total = None
    for t in (0, 1):
        right = jnp.concatenate([w[t, plane, a, b] for a, b in places], axis=0)
        term = lax.dot_general(
            cot[:, t * kv:(t + 1) * kv], right, (((1,), (1,)), ((), ())),
            preferred_element_type=F32,
        )
        total = term if total is None else total + term
    last[...] = total.astype(BF16)
    for k, (a, b) in enumerate(places):
        put(last.at[:, k * rows:(k + 1) * rows], igrad_hbm.at[0, :, block(a, b)])

    tokens = act.shape[0] * 32
    for t in (0, 1):
        total = mine[t] + got_pb[t, 0].astype(F32) + got_pb[t, 1].astype(F32)
        at = slice(t * kv, (t + 1) * kv)
        new_master[:, at], new_first[:, at], new_second[:, at] = adam_update(
            master[0, :, at], first[0, :, at], second[0, :, at],
            total.T * (1.0 / math.sqrt(tokens)),
        )
        for src, dst in (
            (new_master, master_hbm), (new_first, first_hbm), (new_second, second_hbm)
        ):
            put(src.at[:, at], dst.at[0, :, at])
    for copy in started:
        copy.wait()


def finish(tok, kv2, rows, *held):
    igrad, master, first, second, outer, moment = held[:6]
    hbm = pl.BlockSpec(memory_space=pl.ANY)
    results = [jax.ShapeDtypeStruct((1, tok, kv2), BF16)]
    results += [
        jax.ShapeDtypeStruct(r.shape, r.dtype)
        for r in (igrad, master, first, second, outer, moment)
    ]
    return pl.pallas_call(
        finish_kernel,
        out_shape=tuple(results),
        in_specs=[pl.BlockSpec(memory_space=pltpu.VMEM)] * len(held),
        out_specs=(hbm,) * len(results),
        scratch_shapes=[
            pltpu.VMEM((tok, kv2), BF16),
            pltpu.VMEM((tok, 2 * rows), BF16),
            pltpu.VMEM((rows, kv2), F32),
            pltpu.VMEM((rows, kv2), F32),
            pltpu.VMEM((rows, kv2), F32),
            pltpu.SemaphoreType.DMA((21,)),
        ],
        compiler_params=pltpu.CompilerParams(vmem_limit_bytes=16 * 2**20),
        name="finish",
    )(*held)


def train_step(activations, cotangent, master, outer, local, moment, first, second):
    tok, width = activations.shape[1:]
    kv2 = cotangent.shape[2]
    rows = master.shape[1]
    kv, kh = kv2 // 2, kv2 // 4
    dma = pltpu.SemaphoreType.DMA
    sems = []
    for shape in ((2, 2), (2, 2), (2, 4), (2, 8, 2), (2, 8, 2)):
        sems += [dma(shape), dma(shape)]
    for shape in ((2, 8, 2), (2, 8, 2), (2, 4), (2, 2), (2, 2)):
        sems += [dma(shape), dma(shape)]
    for shape in ((3,), (2, 4), (2, 4)):
        sems += [dma(shape), dma(shape)]
    layer = outer.shape[1:]
    hbm = pl.BlockSpec(memory_space=pl.ANY)
    return pl.pallas_call(
        train_kernel,
        out_shape=(
            pltpu.VMEM((1, tok, width), BF16),
            pltpu.VMEM((1, rows, kv2), F32),
            pltpu.VMEM((1, rows, kv2), F32),
            pltpu.VMEM((1, rows, kv2), F32),
            pltpu.VMEM(outer.shape, F32),
            pltpu.VMEM(outer.shape, F32),
            pltpu.VMEM((tok, width), BF16),
            pltpu.VMEM((tok, kv2), BF16),
            pltpu.VMEM((2, 2, N, N, rows, kv), BF16),
            pltpu.VMEM((2, tok, kv), F32),
            pltpu.VMEM((2, kv, rows), F32),
            pltpu.VMEM((2, 2, kv, rows), BF16),
        ),
        in_specs=[hbm] * 8,
        out_specs=tuple(pl.BlockSpec(memory_space=pltpu.VMEM) for _ in range(12)),
        scratch_shapes=[
            pltpu.VMEM((kv2, tok), BF16),
            pltpu.VMEM((2, 8, 4, kv, rows), BF16),
            pltpu.VMEM((2, 8, 2, kv - kv // 4, rows), BF16),
            pltpu.VMEM((2, 8, 2, kv, rows), BF16),
            pltpu.VMEM((2, 4, N, REDUCE_EARLY, rows), BF16),
            pltpu.VMEM((2, 4, kv - REDUCE_EARLY, rows), BF16),
            pltpu.VMEM((2, 2, kh, rows), BF16),
            pltpu.VMEM((2, *layer), F32),
            pltpu.VMEM(layer, BF16),
            pltpu.VMEM(layer, BF16),
            pltpu.VMEM(layer, BF16),
            pltpu.VMEM(layer, BF16),
            pltpu.VMEM((2, *layer), F32),
            dma((10,)),
            *sems,
        ],
        compiler_params=pltpu.CompilerParams(
            collective_id=0, has_side_effects=True, vmem_limit_bytes=30 * 2**20
        ),
        cost_estimate=pl.CostEstimate(
            flops=6 * tok * width * kv2, bytes_accessed=100 * 2**20, transcendentals=0
        ),
        name="train_step",
    )(activations, cotangent, master, outer, local, moment, first, second)


def shards(
    activations,
    kv_cotangent,
    kv_master,
    kv_first,
    kv_second,
    outer_params,
    local_params,
    outer_momentum,
):
    held = train_step(
        activations, kv_cotangent, kv_master, outer_params, local_params, outer_momentum,
        kv_first, kv_second,
    )
    return finish(activations.shape[1], kv_cotangent.shape[2], kv_master.shape[1], *held)


def solution(mesh):
    row_split = P("replica", "fsdp", None)
    fragment = P(None, "fsdp", None)
    return jax.shard_map(
        shards,
        mesh=mesh,
        in_specs=(
            row_split,
            row_split,
            row_split,
            row_split,
            row_split,
            fragment,
            P("replica", None, "fsdp", None),
            fragment,
        ),
        out_specs=(row_split, row_split, row_split, row_split, row_split, fragment, fragment),
        check_vma=False,
    )
```
